512 devices in a mesh: ibpa: 8 (over y), dom: 64 (over z, x, core).
Axes of the slice: x: 4, y: 8, z: 8, core: 2. Of those that a mesh axis runs over, the one named last changes fastest.
Arguments:
- initial_state: float32 [80, 8, 256, 512], P('ibpa', None, 'dom'), parts along dimension 0, may hold values from -6 to 6
- source: float32 [80, 8, 256, 512], P('ibpa', None, 'dom'), parts along dimension 0, may hold values from -6 to 6
- field_coupling: float32 [5, 5], replicated, may hold values from -2.5 to 2.5
- frequency: float32 [1], replicated, may hold values from 0.5 to 2
- phase_angle: float32 [8], P('ibpa'), parts along dimension 0, may hold values from -3.140625 to 3.140625
- face_owner: int32 [4096, 1], P('dom'), may hold values from 0 to 63; in each aligned block of 64 rows (0 to 63, 64 to 127, ...) at most 2 rows name the same one
- face_slot: int32 [4096], P('dom'), may hold values from 0 to 31
- radial_basis: float32 [256, 256], replicated, may hold values from -0.375 to 0.375
- cycle_coupling: float32 [2, 5, 5], replicated, may hold values from -2.5 to 2.5
- cycle_gain: float32 [2, 5, 256, 512], P(None, None, None, 'dom'), may hold values from 0.05 to 1
Outputs:
- relaxed: float32 [80, 8, 256, 512], P('ibpa', None, 'dom'), parts along dimension 0
- residual: float32 [80, 8, 256, 512], P('ibpa', None, 'dom'), parts along dimension 0
The draws below stay inside these ranges and needn't reach their ends.
There are 8 independent parts, one for each index of `ibpa`. The reference program is written for one: setup_inputs(seed, part) draws one part's arguments, and reference() takes and returns one part's arrays. A program takes and returns all parts, laid end to end along the dimension named above; an argument that names none is the same for every part. Nothing has to cross between parts.
Inputs may be any that keep to these rules, and one draw needn't show every extreme that they name: `face_owner`: among the 64 faces of one device no owner rank appears more than 2 times, and in some device one appears exactly 2 times.
All inputs are finite; a program needn't handle non-finite values.
Results may differ from the reference program's by a relative error of at most 0.0001.
Values sent between devices are 32-bit elements; how exact they have to be, the bound alone decides.
A program may use at most 64 MiB of HBM per device.

```python
import math
import jax
import jax.numpy as jnp
import numpy as np
from jax import lax

AX = 8
RAD_DEV = 4
AZI = 512
SWEEPS = 2
RAD = 256
FACES_DEV = 64
FACES = 4096
CAP = 2
N_DOM = 64


def with_ends(entries, stream_key, smallest, largest):
    longest = entries.shape.index(max(entries.shape))
    spots = []
    for shift in (0, 1):
        where = [jax.random.randint(jax.random.fold_in(stream_key, axis), (), 0, length) for axis, length in enumerate(entries.shape)]
        where[longest] = (where[longest] + shift) % entries.shape[longest]
        spots.append(tuple(where))
    return entries.at[spots[0]].set(smallest).at[spots[1]].set(largest)


def steps_of(stream_key, shape, split, least, top_value):
    gain = 1.0
    for position, shards_of in split:
        draws = jax.random.uniform(jax.random.fold_in(jax.random.fold_in(stream_key, 6), position), (shards_of,), jnp.float32, least / len(split), top_value / len(split))
        gain = gain * jnp.repeat(jnp.exp(draws), shape[position] // shards_of).reshape((-1,) + (1,) * (len(shape) - 1 - position))
    return gain


def assign_block(stream_key, own, number, rows, count, top, most, slope):
    order = jax.random.permutation(stream_key, count)
    crowded, usual = shares(count, rows * top, most, slope, True), shares(count, rows * top, most, slope, False)
    places = jnp.arange(count)

    def named(sizes, turn):
        used = int((sizes > 0).sum())
        fixed = max(1, used // 4)
        moved = fixed + (places - fixed + turn * (used - fixed)) % max(1, count - fixed)
        return jnp.zeros((count,), jnp.int32).at[order[jnp.where(places < fixed, places, moved)]].set(jnp.asarray(sizes, jnp.int32))

    sizes = jnp.where(number % 4 == 0, named(crowded, number // 4), named(usual, number - number // 4 - 1))
    mixed = jax.random.permutation(jax.random.fold_in(own, 3), count)
    giver, receiver = mixed[0:count // 2 * 2:2], mixed[1:count // 2 * 2:2]
    room = jnp.minimum(sizes[giver] - 1, most - sizes[receiver]) // 2
    room = jnp.where((giver == order[0]) | (receiver == order[0]) | (sizes[receiver] == 0), 0, jnp.maximum(room, 0))
    moved = jax.random.randint(jax.random.fold_in(own, 4), (count // 2,), 0, 1 << 20) % (room + 1)
    sizes = sizes.at[giver].add(-moved).at[receiver].add(moved)
    items = jnp.searchsorted(jnp.cumsum(sizes), jnp.arange(rows * top), side="right").astype(jnp.int32)
    listing = items.reshape(top, rows).T
    listing = listing[jax.random.permutation(jax.random.fold_in(own, 1), rows)]
    turn = jax.random.randint(jax.random.fold_in(own, 2), (rows, 1), 0, top)
    return jnp.take_along_axis(listing, (jnp.arange(top)[None, :] + turn) % top, axis=1)


def shares(number_of, total, reach, lean, full):
    loads = [(1 << 20) // math.isqrt(grade ** lean) + 1 for grade in range(1, number_of + 1)]
    largest = reach if full else min(reach, max(-(-total // number_of), total * loads[0] // sum(loads)))
    least = 1 if total - largest >= number_of - 1 else 0
    holding, spare = [largest] + [least] * (number_of - 1), total - largest - least * (number_of - 1)
    while spare > 0:
        free = [i for i in range(1, number_of) if holding[i] < largest] or [i for i in range(1, number_of) if holding[i] < reach]
        mass, remaining = sum([loads[i] for i in free]), spare
        for i in free:
            more = min(reach - holding[i], max(1, remaining * loads[i] // mass), spare)
            holding[i] = holding[i] + more
            spare = spare - more
    return np.array(holding)


def normal_values(stream_key, extent, deviation, reach, cuts=(), kind=jnp.bfloat16):
    level = steps_of(stream_key, extent, cuts, -0.22, 0.18) if cuts else 1.0
    entries = jax.random.normal(stream_key, extent, jnp.float32) * deviation * level
    return jnp.minimum(jnp.maximum(entries, -reach), reach).astype(kind)


def setup_inputs(seed: int = 0, part: int = 0) -> dict:
    key_of = jax.random.split(jax.random.key(seed), 11)
    part_keys = jax.random.split(jax.random.fold_in(key_of[10], part), 11)
    initial_state = normal_values(part_keys[0], (10, AX, RAD, AZI), 1.0, 6.0, ((2, 64),), jnp.float32)
    source = normal_values(part_keys[1], (10, AX, RAD, AZI), 1.0, 6.0, ((2, 64),), jnp.float32)
    field_coupling = normal_values(key_of[2], (5, 5), 5 ** -0.5, 2.5, (), jnp.float32)
    frequency = jnp.clip(jax.random.uniform(key_of[3], (1,), jnp.float32, 0.5, 2.0), 0.5, 2.0)
    phase_angle = jnp.clip(jax.random.uniform(part_keys[4], (1,), jnp.float32, -3.140625, 3.140625), -3.140625, 3.140625)
    face_owner_keys = jax.random.split(jax.random.fold_in(key_of[5], 1), FACES // FACES_DEV)
    face_owner_turns = jax.random.permutation(jax.random.fold_in(key_of[5], 3), FACES // FACES_DEV)
    face_owner = jax.vmap(lambda own, number: assign_block(jax.random.fold_in(key_of[5], 2), own, number, FACES_DEV, N_DOM, 1, CAP, 2))(face_owner_keys, face_owner_turns).reshape((FACES, 1))
    face_slot = with_ends(jax.random.randint(key_of[6], (FACES,), 0, AX * RAD_DEV), jax.random.fold_in(key_of[6], 1), 0, (AX * RAD_DEV) - 1).astype(jnp.int32)
    radial_basis = normal_values(key_of[7], (RAD, RAD), RAD ** -0.5, 0.375, (), jnp.float32)
    cycle_coupling = normal_values(key_of[8], (2, 5, 5), 5 ** -0.5, 2.5, (), jnp.float32)
    cycle_gain = jnp.clip(jnp.exp(math.log(1.0) - 2.9957323 * jax.random.uniform(key_of[9], (2, 5, RAD, AZI), jnp.float32) ** steps_of(key_of[9], (2, 5, RAD, AZI), ((3, 64),), -0.2, 0.2)), 0.05, 1.0)
    return {"initial_state": initial_state, "source": source, "field_coupling": field_coupling, "frequency": frequency, "phase_angle": phase_angle, "face_owner": face_owner, "face_slot": face_slot, "radial_basis": radial_basis, "cycle_coupling": cycle_coupling, "cycle_gain": cycle_gain}


precise = lax.Precision.HIGHEST
relaxation = 7.0


def tables(length):
    indices = jnp.arange(length, dtype=jnp.int32)
    product = (indices[:, None] * indices[None, :]) % length
    angles = product.astype(jnp.float32) * (2.0 * math.pi / length)
    return jnp.cos(angles), jnp.sin(angles)


def forward_fourier(real_part, imag_part, cosine_table, sine_table):
    out_real = jnp.matmul(real_part, cosine_table, precision=precise) + jnp.matmul(imag_part, sine_table, precision=precise)
    out_imag = jnp.matmul(imag_part, cosine_table, precision=precise) - jnp.matmul(real_part, sine_table, precision=precise)
    return out_real, out_imag


def inverse_fourier(real_part, imag_part, cosine_table, sine_table):
    length = cosine_table.shape[0]
    out_real = (jnp.matmul(real_part, cosine_table, precision=precise) - jnp.matmul(imag_part, sine_table, precision=precise)) / length
    out_imag = (jnp.matmul(imag_part, cosine_table, precision=precise) + jnp.matmul(real_part, sine_table, precision=precise)) / length
    return out_real, out_imag


def radial_filter(cycle_modes, radial_basis, cycle_coupling, cycle_gain):
    radial = jnp.einsum("kr,xcfrm->xcfkm", radial_basis, cycle_modes, precision=precise)
    blended = jnp.einsum("xgf,xcfkm->xcgkm", cycle_coupling, radial, precision=precise) * cycle_gain[:, None]
    return jnp.einsum("kr,xcgkm->xcgrm", radial_basis, blended, precision=precise)


def apply_phase(values, cos_value, sin_value, direction):
    real_part, imag_part = values[:5], values[5:]
    return jnp.concatenate([cos_value * real_part - direction * sin_value * imag_part,
                            cos_value * imag_part + direction * sin_value * real_part], axis=0)


def operate(current, padded, ghosts, low_inflow, high_inflow, field_coupling, frequency):
    real_part, imag_part = current[:5], current[5:]
    mixed_real = jnp.einsum("gf,fart->gart", field_coupling, real_part, precision=precise)
    mixed_imag = jnp.einsum("gf,fart->gart", field_coupling, imag_part, precision=precise)
    center = 6.0 * current + jnp.concatenate([mixed_real - frequency * imag_part, mixed_imag + frequency * real_part], axis=0)
    ahead = jnp.concatenate([current[:, 1:], ghosts[1][:, None]], axis=1)
    behind = jnp.concatenate([ghosts[0][:, None], current[:, :-1]], axis=1)
    radial_sum = padded[:, :, 2:] + padded[:, :, :-2]
    after_az = jnp.concatenate([current[..., 1:], high_inflow[..., None]], axis=3)
    before_az = jnp.concatenate([low_inflow[..., None], current[..., :-1]], axis=3)
    return center - (ahead + behind + radial_sum + after_az + before_az)


def cycle_ghosts(current, radial_basis, cycle_coupling, cycle_gain, cosine_table, sine_table):
    cycle_data = jnp.stack([current[:, 0], current[:, -1]])
    mode_real, mode_imag = forward_fourier(cycle_data[:, :5], cycle_data[:, 5:], cosine_table, sine_table)
    cycle_modes = jnp.stack([mode_real, mode_imag], axis=1)
    returned = radial_filter(cycle_modes, radial_basis, cycle_coupling, cycle_gain)
    ghost_real, ghost_imag = inverse_fourier(returned[:, 0], returned[:, 1], cosine_table, sine_table)
    return jnp.concatenate([ghost_real, ghost_imag], axis=1)


def partners(current, face_owner, face_slot):
    strip_len = AX * RAD_DEV
    low_strip = current[:, :, :, 0].reshape(10, AX, N_DOM, RAD_DEV).transpose(2, 0, 1, 3).reshape(N_DOM, 10, strip_len)
    high_strip = current[:, :, :, -1].reshape(10, AX, N_DOM, RAD_DEV).transpose(2, 0, 1, 3).reshape(N_DOM, 10, strip_len)
    strips = jnp.concatenate([low_strip, high_strip], axis=2)
    owners = face_owner[:, 0].astype(jnp.int32)
    local = jnp.arange(owners.shape[0], dtype=jnp.int32) % (2 * strip_len)
    sides = local // strip_len
    column = ((1 - sides) * strip_len + face_slot).astype(jnp.int32)
    partner = strips[owners, :, column]
    partner = partner.reshape(N_DOM, 2, AX, RAD_DEV, 10).transpose(1, 4, 2, 0, 3)
    return partner.reshape(2, 10, AX, N_DOM * RAD_DEV)


def reference(initial_state, source, field_coupling, frequency, phase_angle, face_owner, face_slot, radial_basis, cycle_coupling, cycle_gain):
    cosine_table, sine_table = tables(AZI)
    cos_value = jnp.cos(phase_angle[0])
    sin_value = jnp.sin(phase_angle[0])
    current = initial_state
    residual = jnp.zeros_like(initial_state)
    for sweep_index in range(SWEEPS):
        ghosts = cycle_ghosts(current, radial_basis, cycle_coupling, cycle_gain, cosine_table, sine_table)
        partner = partners(current, face_owner, face_slot)
        low_inflow = apply_phase(partner[0], cos_value, sin_value, -1.0)
        high_inflow = apply_phase(partner[1], cos_value, sin_value, 1.0)
        padded = jnp.pad(current, ((0, 0), (0, 0), (1, 1), (0, 0)))
        image = operate(current, padded, ghosts, low_inflow, high_inflow, field_coupling, frequency[0])
        residual = source - image
        current = current + residual / relaxation
    return current, residual
```

```python
import functools

import jax
import jax.numpy as jnp
import ml_dtypes
import numpy as np
from jax import lax
from jax.experimental import pallas as pl
from jax.experimental.pallas import tpu as pltpu

F32 = jnp.float32
BF16 = jnp.bfloat16
AX = 8
RD = 4
MODES = 8
LINE = 80
OWN = LINE
PAD = 24
UPPER = OWN + RD * LINE + PAD
ROWS = UPPER + LINE
MESH = pl.DeviceIdType.MESH


@functools.lru_cache(None)
def fourier_tables(count):
    azi = MODES * count
    quarter = azi // 4
    kk, e = np.arange(quarter) // count, np.arange(quarter) % count
    k = 2 * e + kk
    t = np.arange(quarter)
    ahead, back = [], []
    for b in range(4):
        angle = ((4 * k + b)[:, None] * t[None, :]) % azi * (2 * np.pi / azi)
        ahead.append(np.concatenate([np.cos(angle), np.sin(angle)], axis=1))
        back.append(np.concatenate([np.cos(angle), np.sin(angle)], axis=0) / azi)

    def split(x):
        x = x.astype(np.float32)
        hi = x.astype(ml_dtypes.bfloat16)
        lo = (x - hi.astype(np.float32)).astype(ml_dtypes.bfloat16)
        return np.stack([hi, lo])

    return split(np.stack(ahead)), split(np.stack(back))


def split(x):
    hi = x.astype(BF16)
    return hi, (x - hi.astype(F32)).astype(BF16)


def dot3(a, b, contract=((1,), (0,))):
    dims = (contract, ((), ()))

    def one(u, v):
        return lax.dot_general(u, v, dims, preferred_element_type=F32)

    return one(a[0], b[0]) + (one(a[1], b[0]) + one(a[0], b[1]))


def get(ref, rows):
    return jnp.concatenate([ref[tile, rows, :] for tile in range(ref.shape[0])], axis=1)


def put(ref, rows, value):
    for tile in range(ref.shape[0]):
        ref[tile, rows, :] = value[:, tile * 128 : (tile + 1) * 128]


def rolled(x, shift):
    shift = shift % 128
    return x if shift == 0 else pltpu.roll(x, shift, 1)


def kernel(
    n,
    wide,
    state_hbm,
    source_hbm,
    gain_hbm,
    basis_hbm,
    ahead_hbm,
    back_hbm,
    mix_ref,
    frequency_ref,
    phase_ref,
    owner_ref,
    slot_ref,
    cycle_ref,
    relaxed_hbm,
    residual_hbm,
    stage,
    stage_source,
    gain,
    basis,
    ahead,
    back,
    s0,
    s1,
    source,
    res,
    basis_hi,
    basis_lo,
    turned_hi,
    turned_lo,
    gain_rows,
    strips0,
    strips1,
    inflow,
    modes_out,
    modes_in,
    late_out,
    late_in,
    first_out,
    first_in,
    second_out,
    second_in,
    packed,
    ghosts,
    load_sem,
    a2a_send,
    a2a_recv,
    strip_send,
    strip_recv,
    halo_send,
    halo_recv,
):
    azi = MODES * n
    quarter = azi // 4
    rad = RD * n
    nz = n // wide
    me = lax.axis_index("dom")
    my_z, my_w = me // wide, me % wide
    barrier = pltpu.get_barrier_semaphore()

    def load(i, src, dst):
        return pltpu.make_async_copy(src, dst, load_sem.at[i])

    loads = [
        load(0, state_hbm, stage),
        load(1, ahead_hbm, ahead),
        load(2, source_hbm, stage_source),
        load(3, basis_hbm, basis),
        load(4, gain_hbm, gain),
        load(5, back_hbm, back),
    ]
    for copy in loads:
        copy.start()

    def greet(s, carry):
        pl.semaphore_signal(
            barrier, inc=1, device_id={"dom": (me + s) % n}, device_id_type=MESH
        )
        return carry

    lax.fori_loop(1, n, greet, 0)

    lane = lax.broadcasted_iota(jnp.int32, (1, 128), 1)
    row8 = lax.broadcasted_iota(jnp.int32, (8, 128), 0)
    lane8 = lax.broadcasted_iota(jnp.int32, (8, 128), 1)

    def exchange(i, out, into):
        def send(s, carry):
            peer = (me + s) % n
            pltpu.make_async_remote_copy(
                src_ref=out.at[pl.ds(pl.multiple_of(peer * 8, 8), 8)],
                dst_ref=into.at[pl.ds(pl.multiple_of(me * 8, 8), 8)],
                send_sem=a2a_send.at[i],
                recv_sem=a2a_recv.at[i],
                device_id={"dom": peer},
                device_id_type=MESH,
            ).start()
            return carry

        lax.fori_loop(1, n, send, 0)
        mine = pl.ds(pl.multiple_of(me * 8, 8), 8)
        into[mine, :] = out[mine, :]

    def arrived(sem, ref):
        pltpu.make_async_copy(ref, ref, sem).wait()

    def exchange_wait(i, into):
        arrived(a2a_recv.at[i], into.at[pl.ds(0, (n - 1) * 8)])

    def strip_z(i, strips):
        mine = pl.ds(pl.multiple_of((my_w * nz + my_z) * 8, 8), 8)

        def send(s, carry):
            peer = (my_z + s) % nz * wide + my_w
            pltpu.make_async_remote_copy(
                src_ref=strips.at[mine],
                dst_ref=strips.at[mine],
                send_sem=strip_send.at[2 * i],
                recv_sem=strip_recv.at[2 * i],
                device_id={"dom": peer},
                device_id_type=MESH,
            ).start()
            return carry

        lax.fori_loop(1, nz, send, 0)

    def strip_w(i, strips):
        arrived(strip_recv.at[2 * i], strips.at[pl.ds(0, (nz - 1) * 8)])
        mine = pl.ds(pl.multiple_of(my_w * nz * 8, 8), nz * 8)

        def send(s, carry):
            peer = my_z * wide + (my_w + s) % wide
            pltpu.make_async_remote_copy(
                src_ref=strips.at[mine],
                dst_ref=strips.at[mine],
                send_sem=strip_send.at[2 * i + 1],
                recv_sem=strip_recv.at[2 * i + 1],
                device_id={"dom": peer},
                device_id_type=MESH,
            ).start()
            return carry

        lax.fori_loop(1, wide, send, 0)

    def strip_wait(i, strips):
        arrived(strip_recv.at[2 * i + 1], strips.at[pl.ds(0, (wide - 1) * nz * 8)])

    def halo_copies(i, low_src, low_dst, up_src, up_dst):
        down = pltpu.make_async_remote_copy(
            src_ref=low_src,
            dst_ref=up_dst,
            send_sem=halo_send.at[2 * i],
            recv_sem=halo_recv.at[2 * i],
            device_id={"dom": jnp.maximum(me - 1, 0)},
            device_id_type=MESH,
        )
        up = pltpu.make_async_remote_copy(
            src_ref=up_src,
            dst_ref=low_dst,
            send_sem=halo_send.at[2 * i + 1],
            recv_sem=halo_recv.at[2 * i + 1],
            device_id={"dom": jnp.minimum(me + 1, n - 1)},
            device_id_type=MESH,
        )
        return down, up

    def halo_start(copies):
        @pl.when(me > 0)
        def _():
            copies[0].start()

        @pl.when(me < n - 1)
        def _():
            copies[1].start()

    def halo_recv_wait(copies):
        @pl.when(me < n - 1)
        def _():
            copies[0].wait_recv()

        @pl.when(me > 0)
        def _():
            copies[1].wait_recv()

    def halo_send_wait(copies):
        @pl.when(me > 0)
        def _():
            copies[0].wait_send()

        @pl.when(me < n - 1)
        def _():
            copies[1].wait_send()

    def line_halo(i, s):
        return halo_copies(
            i,
            s.at[:, pl.ds(OWN, LINE)],
            s.at[:, pl.ds(0, LINE)],
            s.at[:, pl.ds(OWN + 3 * LINE, LINE)],
            s.at[:, pl.ds(UPPER, LINE)],
        )

    def spread(staged, dst, first):
        def body(cf, carry):
            for a in range(AX):
                put(dst, pl.ds(first + cf * 8 + a, RD, stride=LINE), staged[cf, a])
            return carry

        lax.fori_loop(0, 10, body, 0)

    def collect(src, staged):
        def body(cf, carry):
            for a in range(AX):
                staged[cf, a] = get(src, pl.ds(cf * 8 + a, RD, stride=LINE))
            return carry

        lax.fori_loop(0, 10, body, 0)

    def make_strip(s, strips):
        def body(r, acc):
            base = pl.multiple_of(OWN + r * LINE, 8)
            part = jnp.zeros((8, 128), F32)
            for cf in range(10):
                ends = jnp.where(
                    lane8 == 0,
                    s[0, pl.ds(base + cf * 8, 8), :],
                    s[s.shape[0] - 1, pl.ds(base + cf * 8, 8), :],
                )
                part = jnp.where(lane8 // 2 == cf * 4, rolled(ends, cf * 8 + 1), part)
            part = pltpu.roll(part, 2 * r, 1)
            return jnp.where(lane8 % 8 // 2 == r, part, acc)

        tile = lax.fori_loop(0, RD, body, jnp.zeros((8, 128), F32))
        mine = pl.ds(pl.multiple_of((my_w * nz + my_z) * 8, 8), 8)
        strips[mine, :] = tile

    angle = jnp.broadcast_to(phase_ref[0], (8, 128))
    cos_value, sin_value = jnp.cos(angle), jnp.sin(angle)

    def make_inflow(strips):
        def body(a, acc):
            for side in range(2):
                for r in range(RD):
                    face = side * AX * RD + a * RD + r
                    owner = owner_ref[face]
                    slot = slot_ref[face]
                    tile = owner % wide * nz + owner // wide
                    entry = strips[pl.ds(tile * 8 + slot // RD, 1), :]
                    shift = 2 * (r - slot % RD) + 1 - 2 * side + 128
                    moved = pltpu.roll(jnp.broadcast_to(entry, (8, 128)), shift, 1)
                    here = (row8 == a) & (lane8 % 8 == 2 * r + 1 - side)
                    acc = jnp.where(here, moved, acc)
            return acc

        partner = lax.fori_loop(0, AX, body, jnp.zeros((8, 128), F32))
        other = jnp.where(lane8 < 40, rolled(partner, -40), rolled(partner, 40))
        plus = (lane8 < 40) == (lane8 % 2 == 1)
        inflow[...] = cos_value * partner + jnp.where(plus, sin_value, -sin_value) * other

    def mixes(g, x):
        total = mix_ref[g, 0] * x[0]
        for f in range(1, 5):
            total = total + mix_ref[g, f] * x[f]
        return total

    frequency = frequency_ref[0]
    first_lane = lax.broadcasted_iota(jnp.int32, (8, azi), 1) == 0
    last_lane = lax.broadcasted_iota(jnp.int32, (8, azi), 1) == azi - 1
    row = lax.broadcasted_iota(jnp.int32, (8, azi), 0)

    def sweep(s, emit):
        def body(r, carry):
            base = pl.multiple_of(OWN + r * LINE, 8)
            above = pl.multiple_of(base + LINE + r // 3 * PAD, 8)
            here = pltpu.roll(inflow[...], 128 - 2 * r, 1)
            x = [get(s, pl.ds(base + cf * 8, 8)) for cf in range(10)]
            for c in range(2):
                for g in range(5):
                    cf = 5 * c + g
                    mine = x[cf]
                    other = x[5 * (1 - c) + g]
                    turn = frequency * other
                    center = 6.0 * mine + mixes(g, x[5 * c : 5 * c + 5])
                    center = center - turn if c == 0 else center + turn
                    along = jnp.where(row == 7, 0.0, pltpu.roll(mine, 7, 0)) + jnp.where(
                        row == 0, 0.0, pltpu.roll(mine, 1, 0)
                    )
                    lines = get(s, pl.ds(base - LINE + cf * 8, 8)) + get(
                        s, pl.ds(above + cf * 8, 8)
                    )
                    ends = rolled(here, -(cf * 8 + 1))
                    ends = jnp.concatenate([ends] * (azi // 128), axis=1)
                    after = jnp.where(last_lane, ends, pltpu.roll(mine, azi - 1, 1))
                    before = jnp.where(first_lane, ends, pltpu.roll(mine, 1, 1))
                    at = pl.multiple_of(r * LINE, 8) + cf * 8
                    image = center - (along + lines + (after + before))
                    emit(at, mine, get(source, pl.ds(at, 8)) - image)
            return carry

        lax.fori_loop(0, RD, body, 0)

    def forward(s, out):
        halves = []
        for c in range(2):
            blocks = [
                get(s, pl.ds(OWN + r * LINE + c * 40 + 7 * x, 8, stride=8))
                for r in range(RD)
                for x in range(2)
            ]
            halves.append(jnp.concatenate(blocks, axis=0))
        re, im = ([h[:, a * quarter : (a + 1) * quarter] for a in range(4)] for h in halves)
        se, de, so, do = re[0] + re[2], re[0] - re[2], re[1] + re[3], re[1] - re[3]
        te, ue, to, uo = im[0] + im[2], im[0] - im[2], im[1] + im[3], im[1] - im[3]
        classes = [(se + so, te + to), (de + uo, ue - do), (se - so, te - to), (de - uo, ue + do)]
        modes = [None] * MODES
        for b, (yr, yi) in enumerate(classes):
            y = jnp.concatenate(
                [jnp.concatenate([yr, yi], axis=0), jnp.concatenate([yi, -yr], axis=0)], axis=1
            )
            z = dot3((ahead[0, b], ahead[1, b]), split(y), ((1,), (1,)))
            modes[b], modes[4 + b] = z[:n], z[n:]
        for f in range(5):
            part = rolled(modes[0], -f)
            for j in range(1, MODES):
                part = jnp.where(lane % 8 == j, rolled(modes[j], j - f), part)
            out[pl.ds(f, n, stride=8), :] = part

    def cycle_weight(g, f):
        return jnp.where(lane // 8 % 2 == 0, cycle_ref[g * 5 + f], cycle_ref[25 + g * 5 + f])

    block = lane // 16 % 4

    def filtered(modes):
        blended = []
        for g in range(5):
            total = cycle_weight(g, 0) * modes[0]
            for f in range(1, 5):
                total = total + cycle_weight(g, f) * modes[f]
            blended.append(total)
        for r in range(RD):
            part = rolled(blended[0], -16 * r)
            for g in range(1, 4):
                part = jnp.where(block == g, rolled(blended[g], 16 * (g - r)), part)
            packed[0, pl.ds(r, n, stride=RD), :] = part
            packed[1, pl.ds(r, n, stride=RD), :] = rolled(blended[4], -16 * r)
        x = jnp.concatenate([packed[0], packed[1]], axis=1)
        radial = dot3((basis_hi[...], basis_lo[...]), split(x))
        radial = radial * gain_rows[...]
        back_r = dot3((turned_hi[...], turned_lo[...]), split(radial))
        packed[0] = back_r[:, :128]
        packed[1] = back_r[:, 128:]
        lines0 = [packed[0, pl.ds(r, n, stride=RD), :] for r in range(RD)]
        lines1 = [packed[1, pl.ds(r, n, stride=RD), :] for r in range(RD)]
        result = []
        for g in range(5):
            lines, place = (lines0, g) if g < 4 else (lines1, 0)
            part = rolled(lines[0], -16 * place)
            for r in range(1, RD):
                part = jnp.where(block == r, rolled(lines[r], 16 * (r - place)), part)
            result.append(part)
        return result

    def inverse(modes):
        spread_modes = [modes[pl.ds(g, n, stride=8), :] for g in range(5)]
        z = []
        for j in range(MODES):
            part = rolled(spread_modes[0], -j)
            for g in range(1, 5):
                part = jnp.where(lane % 8 == g, rolled(spread_modes[g], g - j), part)
            z.append(part)
        v = []
        for b in range(4):
            turned = jnp.concatenate([z[b], z[4 + b]], axis=0).T
            y = jnp.concatenate(
                [turned, jnp.concatenate([-turned[64:], turned[:64]], axis=0)], axis=1
            )
            v.append(dot3(split(y), (back[0, b], back[1, b])))
        s, d, p, q = v[0] + v[2], v[0] - v[2], v[1] + v[3], v[1] - v[3]
        iq = jnp.concatenate([-q[64:], q[:64]], axis=0)
        points = jnp.concatenate([s + p, d + iq, s - p, d - iq], axis=1)
        for c in range(2):
            for r in range(RD):
                put(
                    ghosts,
                    pl.ds(r * 32 + c * 16, 16),
                    points[c * 64 + r * 16 : c * 64 + r * 16 + 16],
                )

    def add_ghosts(dst, first, values, start, scale):
        for c in range(2):
            for x in range(2):
                rows = pl.ds(first + c * 40 + 7 * x, 5, stride=8)
                ghost = get(values, pl.ds(start + c * 16 + x * 8, 8))[:5]
                put(dst, rows, get(dst, rows) + scale * ghost)

    seventh = 1.0 / 7.0
    loads[0].wait()
    spread(stage, s0, OWN)
    for s in (s0, s1):
        put(s, pl.ds(OWN + RD * LINE, PAD), jnp.zeros((PAD, azi), F32))

    @pl.when(me == 0)
    def _():
        for s in (s0, s1):
            put(s, pl.ds(0, LINE), jnp.zeros((LINE, azi), F32))

    @pl.when(me == n - 1)
    def _():
        for s in (s0, s1):
            put(s, pl.ds(UPPER, LINE), jnp.zeros((LINE, azi), F32))

    make_strip(s0, strips0)
    pl.semaphore_wait(barrier, n - 1)
    strip_z(0, strips0)
    halo0 = line_halo(0, s0)
    halo_start(halo0)

    loads[1].wait()
    forward(s0, modes_out)
    strip_w(0, strips0)
    exchange(0, modes_out, modes_in)

    loads[2].wait()
    spread(stage_source, source, 0)
    loads[3].wait()
    whole = basis[...]
    basis_hi[...], basis_lo[...] = split(whole)
    turned_hi[...], turned_lo[...] = split(whole.T)
    loads[4].wait()
    rows0 = [gain[x, g] for c in range(2) for g in range(4) for x in range(2)]
    rows1 = [gain[x, 4] for c in range(2) for g in range(4) for x in range(2)]
    gain_rows[:, :128] = jnp.concatenate(rows0, axis=0).T
    gain_rows[:, 128:] = jnp.concatenate(rows1, axis=0).T
    loads[5].wait()

    strip_wait(0, strips0)
    make_inflow(strips0)
    halo_recv_wait(halo0)

    def emit_base(at, mine, value):
        put(s1, pl.ds(OWN + at, 8), mine + value * seventh)

    sweep(s0, emit_base)
    halo1 = line_halo(1, s1)
    forward(s1, late_out)
    exchange(1, late_out, late_in)

    exchange_wait(0, modes_in)
    first = filtered([modes_in[pl.ds(f, n, stride=8), :] for f in range(5)])
    for g in range(5):
        first_out[pl.ds(g, n, stride=8), :] = first[g]
    exchange(2, first_out, first_in)

    exchange_wait(1, late_in)
    second = filtered(
        [
            late_in[pl.ds(f, n, stride=8), :] + seventh * first_out[pl.ds(f, n, stride=8), :]
            for f in range(5)
        ]
    )
    for g in range(5):
        second_out[pl.ds(g, n, stride=8), :] = second[g]
    exchange(3, second_out, second_in)

    exchange_wait(2, first_in)
    inverse(first_in)

    def own_ghosts(r, carry):
        add_ghosts(s1, OWN + r * LINE, ghosts, r * 32, seventh)
        return carry

    lax.fori_loop(0, RD, own_ghosts, 0)
    make_strip(s1, strips1)
    strip_z(1, strips1)
    halo_start(halo1)
    strip_w(1, strips1)
    exchange_wait(3, second_in)
    inverse(second_in)
    halo_recv_wait(halo1)
    strip_wait(1, strips1)
    make_inflow(strips1)

    def emit_residual(at, mine, value):
        put(res, pl.ds(at, 8), value)

    sweep(s1, emit_residual)

    def last_ghosts(r, carry):
        add_ghosts(res, r * LINE, ghosts, r * 32, 1.0)
        return carry

    lax.fori_loop(0, RD, last_ghosts, 0)
    collect(res, stage_source)
    write_residual = pltpu.make_async_copy(stage_source, residual_hbm, load_sem.at[0])
    write_residual.start()

    def relax(i, carry):
        at = pl.multiple_of(i * 16, 8)
        rows = pl.ds(at, 16)
        put(res, rows, get(s1, pl.ds(OWN + at, 16)) + get(res, rows) * seventh)
        return carry

    lax.fori_loop(0, RD * LINE // 16, relax, 0)
    collect(res, stage)
    write_relaxed = pltpu.make_async_copy(stage, relaxed_hbm, load_sem.at[1])
    write_relaxed.start()

    for i, out in enumerate((modes_out, late_out, first_out, second_out)):
        arrived(a2a_send.at[i], out.at[pl.ds(0, (n - 1) * 8)])
    for i, strips in enumerate((strips0, strips1)):
        arrived(strip_send.at[2 * i], strips.at[pl.ds(0, (nz - 1) * 8)])
        arrived(strip_send.at[2 * i + 1], strips.at[pl.ds(0, (wide - 1) * nz * 8)])
    halo_send_wait(halo0)
    halo_send_wait(halo1)
    write_residual.wait()
    write_relaxed.wait()


def on_device(
    n,
    initial_state,
    source,
    field_coupling,
    frequency,
    phase_angle,
    face_owner,
    face_slot,
    radial_basis,
    cycle_coupling,
    cycle_gain,
):
    azi = MODES * n
    rad = RD * n
    quarter = azi // 4
    wide = 8 if n >= 64 else 4
    ahead, back = fourier_tables(n)
    shape = (10, AX, RD, azi)
    hbm = pl.BlockSpec(memory_space=pl.ANY)
    smem = pl.BlockSpec(memory_space=pltpu.SMEM)
    vmem = pltpu.VMEM
    peers = (n * 8, 128)
    return pl.pallas_call(
        functools.partial(kernel, n, wide),
        out_shape=(jax.ShapeDtypeStruct(shape, F32), jax.ShapeDtypeStruct(shape, F32)),
        in_specs=[hbm] * 6 + [smem] * 6,
        out_specs=(hbm, hbm),
        scratch_shapes=[
            vmem(shape, F32),
            vmem(shape, F32),
            vmem((2, 5, MODES, rad), F32),
            vmem((rad, rad), F32),
            vmem((2, 4, quarter, 2 * quarter), BF16),
            vmem((2, 4, 2 * quarter, quarter), BF16),
            vmem((azi // 128, ROWS, 128), F32),
            vmem((azi // 128, ROWS, 128), F32),
            vmem((azi // 128, RD * LINE, 128), F32),
            vmem((azi // 128, RD * LINE, 128), F32),
            vmem((rad, rad), BF16),
            vmem((rad, rad), BF16),
            vmem((rad, rad), BF16),
            vmem((rad, rad), BF16),
            vmem((rad, 256), F32),
            vmem(peers, F32),
            vmem(peers, F32),
            vmem((8, 128), F32),
            *[vmem(peers, F32) for _ in range(8)],
            vmem((2, rad, 128), F32),
            vmem((azi // 128, RD * 32, 128), F32),
            pltpu.SemaphoreType.DMA((6,)),
            pltpu.SemaphoreType.DMA((4,)),
            pltpu.SemaphoreType.DMA((4,)),
            pltpu.SemaphoreType.DMA((4,)),
            pltpu.SemaphoreType.DMA((4,)),
            pltpu.SemaphoreType.DMA((4,)),
            pltpu.SemaphoreType.DMA((4,)),
        ],
        compiler_params=pltpu.CompilerParams(
            collective_id=0, has_side_effects=True, vmem_limit_bytes=40 * 1024 * 1024
        ),
    )(
        initial_state,
        source,
        jnp.transpose(cycle_gain, (0, 1, 3, 2)),
        radial_basis,
        jnp.asarray(ahead),
        jnp.asarray(back),
        field_coupling,
        frequency,
        phase_angle,
        face_owner.reshape(-1),
        face_slot,
        cycle_coupling.reshape(-1),
    )


def solution(mesh):
    P = jax.sharding.PartitionSpec
    state = P("ibpa", None, "dom", None)
    in_specs = (
        state,
        state,
        P(),
        P(),
        P("ibpa"),
        P("dom", None),
        P("dom"),
        P(),
        P(),
        P(None, None, None, "dom"),
    )
    return jax.shard_map(
        functools.partial(on_device, mesh.shape["dom"]),
        mesh=mesh,
        in_specs=in_specs,
        out_specs=(state, state),
        check_vma=False,
    )
```

```python
import functools

import jax
import jax.numpy as jnp
import ml_dtypes
import numpy as np
from jax import lax
from jax.experimental import pallas as pl
from jax.experimental.pallas import tpu as pltpu

F32 = jnp.float32
BF16 = jnp.bfloat16
AX = 8
RD = 4
MODES = 8
LINE = 80
OWN = LINE
PAD = 24
UPPER = OWN + RD * LINE + PAD
ROWS = UPPER + LINE
MESH = pl.DeviceIdType.MESH


@functools.lru_cache(None)
def fourier_tables(count):
    azi = MODES * count
    quarter = azi // 4
    kk, e = np.arange(quarter) // count, np.arange(quarter) % count
    k = 2 * e + kk
    t = np.arange(quarter)
    ahead, back = [], []
    for b in range(4):
        angle = ((4 * k + b)[:, None] * t[None, :]) % azi * (2 * np.pi / azi)
        ahead.append(np.concatenate([np.cos(angle), np.sin(angle)], axis=1))
        back.append(np.concatenate([np.cos(angle), np.sin(angle)], axis=0) / azi)

    def split(x):
        x = x.astype(np.float32)
        hi = x.astype(ml_dtypes.bfloat16)
        lo = (x - hi.astype(np.float32)).astype(ml_dtypes.bfloat16)
        return np.stack([hi, lo])

    return split(np.stack(ahead)), split(np.stack(back))


def split(x):
    hi = x.astype(BF16)
    return hi, (x - hi.astype(F32)).astype(BF16)


def dot3(a, b, contract=((1,), (0,))):
    dims = (contract, ((), ()))

    def one(u, v):
        return lax.dot_general(u, v, dims, preferred_element_type=F32)

    return one(a[0], b[0]) + (one(a[1], b[0]) + one(a[0], b[1]))


def get(ref, rows):
    return jnp.concatenate([ref[tile, rows, :] for tile in range(ref.shape[0])], axis=1)


def put(ref, rows, value):
    for tile in range(ref.shape[0]):
        ref[tile, rows, :] = value[:, tile * 128 : (tile + 1) * 128]


def rolled(x, shift):
    shift = shift % 128
    return x if shift == 0 else pltpu.roll(x, shift, 1)


def kernel(
    n,
    wide,
    state_hbm,
    source_hbm,
    gain_hbm,
    basis_hbm,
    ahead_hbm,
    back_hbm,
    mix_ref,
    frequency_ref,
    phase_ref,
    owner_ref,
    slot_ref,
    cycle_ref,
    relaxed_hbm,
    residual_hbm,
    stage,
    stage_source,
    gain,
    basis,
    ahead,
    back,
    s0,
    s1,
    source,
    res,
    basis_hi,
    basis_lo,
    turned_hi,
    turned_lo,
    gain_rows,
    strips0,
    strips1,
    modes_out,
    modes_in,
    late_out,
    late_in,
    first_out,
    first_in,
    second_out,
    second_in,
    packed,
    ghosts,
    load_sem,
    all_send,
    all_recv,
    group_sent,
    group_recv,
    halo_send,
    halo_recv,
):
    azi = MODES * n
    quarter = azi // 4
    rad = RD * n
    nz = n // wide
    me = lax.axis_index("dom")
    my_z, my_w = me // wide, me % wide
    barrier = pltpu.get_barrier_semaphore()

    lane = lax.broadcasted_iota(jnp.int32, (1, 128), 1)
    row8 = lax.broadcasted_iota(jnp.int32, (8, 128), 0)
    lane8 = lax.broadcasted_iota(jnp.int32, (8, 128), 1)

    def peer_of(i):
        return (me + n // 2 + (i % 2) * ((i + 1) // 2) - (1 - i % 2) * (i // 2)) % n

    def greet(step, carry):
        pl.semaphore_signal(
            barrier, inc=1, device_id={"dom": peer_of(step)}, device_id_type=MESH
        )
        return carry

    lax.fori_loop(0, n - 1, greet, 0)

    def load(i, src, dst):
        return pltpu.make_async_copy(src, dst, load_sem.at[i])

    loads = [
        load(0, state_hbm, stage),
        load(1, ahead_hbm, ahead),
        load(2, source_hbm, stage_source),
        load(3, basis_hbm, basis),
        load(4, gain_hbm, gain),
        load(5, back_hbm, back),
    ]
    for copy in loads:
        copy.start()

    def send_all(i, src_of, dst):
        def send(step, carry):
            peer = peer_of(step)
            pltpu.make_async_remote_copy(
                src_ref=src_of(peer),
                dst_ref=dst,
                send_sem=all_send.at[i],
                recv_sem=all_recv.at[i],
                device_id={"dom": peer},
                device_id_type=MESH,
            ).start()
            return carry

        lax.fori_loop(0, n - 1, send, 0)

    def tile_rows(device, count):
        return pl.ds(pl.multiple_of(device * 8, 8), count)

    def exchange(i, out, into):
        send_all(i, lambda peer: out.at[tile_rows(peer, 5)], into.at[tile_rows(me, 5)])
        into[tile_rows(me, 8), :] = out[tile_rows(me, 8), :]

    def arrived(sem, ref):
        pltpu.make_async_copy(ref, ref, sem).wait()

    def exchange_wait(i, into):
        arrived(all_recv.at[i], into.at[pl.ds(0, (n - 1) * 5)])

    def group_send(i, count, peer_at, block):
        def send(step, carry):
            pltpu.make_async_remote_copy(
                src_ref=block,
                dst_ref=block,
                send_sem=group_sent.at[i],
                recv_sem=group_recv.at[i],
                device_id={"dom": peer_at(step)},
                device_id_type=MESH,
            ).start()
            return carry

        lax.fori_loop(1, count, send, 0)

    my_tile = my_w * nz + my_z

    def strip_z(i, strips):
        block = strips.at[tile_rows(my_tile, 8)]
        group_send(2 * i, nz, lambda step: (my_z + step) % nz * wide + my_w, block)

    def strip_w(i, strips):
        arrived(group_recv.at[2 * i], strips.at[pl.ds(0, (nz - 1) * 8)])
        block = strips.at[tile_rows(my_w * nz, nz * 8)]
        group_send(2 * i + 1, wide, lambda step: my_z * wide + (my_w + step) % wide, block)

    def strip_wait(i, strips):
        arrived(group_recv.at[2 * i + 1], strips.at[pl.ds(0, (wide - 1) * nz * 8)])

    def halo_copies(i, low_src, low_dst, up_src, up_dst):
        down = pltpu.make_async_remote_copy(
            src_ref=low_src,
            dst_ref=up_dst,
            send_sem=halo_send.at[2 * i],
            recv_sem=halo_recv.at[2 * i],
            device_id={"dom": jnp.maximum(me - 1, 0)},
            device_id_type=MESH,
        )
        up = pltpu.make_async_remote_copy(
            src_ref=up_src,
            dst_ref=low_dst,
            send_sem=halo_send.at[2 * i + 1],
            recv_sem=halo_recv.at[2 * i + 1],
            device_id={"dom": jnp.minimum(me + 1, n - 1)},
            device_id_type=MESH,
        )
        return down, up

    def halo_start(copies):
        @pl.when(me > 0)
        def _():
            copies[0].start()

        @pl.when(me < n - 1)
        def _():
            copies[1].start()

    def halo_recv_wait(copies):
        @pl.when(me < n - 1)
        def _():
            copies[0].wait_recv()

        @pl.when(me > 0)
        def _():
            copies[1].wait_recv()

    def halo_send_wait(copies):
        @pl.when(me > 0)
        def _():
            copies[0].wait_send()

        @pl.when(me < n - 1)
        def _():
            copies[1].wait_send()

    def line_halo(i, s):
        return halo_copies(
            i,
            s.at[:, pl.ds(OWN, LINE)],
            s.at[:, pl.ds(0, LINE)],
            s.at[:, pl.ds(OWN + 3 * LINE, LINE)],
            s.at[:, pl.ds(UPPER, LINE)],
        )

    def spread(staged, dst, first):
        def body(cf, carry):
            for a in range(AX):
                put(dst, pl.ds(first + cf * 8 + a, RD, stride=LINE), staged[cf, a])
            return carry

        lax.fori_loop(0, 10, body, 0)

    def collect(src, staged, stations):
        def body(cf, carry):
            for a in stations:
                staged[cf, a] = get(src, pl.ds(cf * 8 + a, RD, stride=LINE))
            return carry

        lax.fori_loop(0, 10, body, 0)

    def make_strip(s, strips):
        def body(r, acc):
            base = pl.multiple_of(OWN + r * LINE, 8)
            part = jnp.zeros((8, 128), F32)
            for cf in range(10):
                ends = jnp.where(
                    lane8 == 0,
                    s[0, pl.ds(base + cf * 8, 8), :],
                    s[s.shape[0] - 1, pl.ds(base + cf * 8, 8), :],
                )
                part = jnp.where(lane8 // 2 == cf * 4, rolled(ends, cf * 8 + 1), part)
            part = pltpu.roll(part, 2 * r, 1)
            return jnp.where(lane8 % 8 // 2 == r, part, acc)

        tile = lax.fori_loop(0, RD, body, jnp.zeros((8, 128), F32), unroll=True)
        strips[tile_rows(my_tile, 8), :] = tile

    angle = jnp.broadcast_to(phase_ref[0], (8, 128))
    cos_value, sin_value = jnp.cos(angle), jnp.sin(angle)

    def make_inflow(strips):
        def body(a, acc):
            for side in range(2):
                for r in range(RD):
                    face = side * AX * RD + a * RD + r
                    owner = owner_ref[face]
                    slot = slot_ref[face]
                    tile = owner % wide * nz + owner // wide
                    entry = strips[pl.ds(tile * 8 + slot // RD, 1), :]
                    shift = 2 * (r - slot % RD) + 1 - 2 * side + 128
                    moved = pltpu.roll(jnp.broadcast_to(entry, (8, 128)), shift, 1)
                    here = (row8 == a) & (lane8 % 8 == 2 * r + 1 - side)
                    acc = jnp.where(here, moved, acc)
            return acc

        partner = lax.fori_loop(0, AX, body, jnp.zeros((8, 128), F32), unroll=True)
        other = jnp.where(lane8 < 40, rolled(partner, -40), rolled(partner, 40))
        plus = (lane8 < 40) == (lane8 % 2 == 1)
        return cos_value * partner + jnp.where(plus, sin_value, -sin_value) * other

    def mixes(g, x):
        total = mix_ref[g, 0] * x[0]
        for f in range(1, 5):
            total = total + mix_ref[g, f] * x[f]
        return total

    frequency = frequency_ref[0]
    first_lane = lax.broadcasted_iota(jnp.int32, (8, azi), 1) == 0
    last_lane = lax.broadcasted_iota(jnp.int32, (8, azi), 1) == azi - 1
    row = lax.broadcasted_iota(jnp.int32, (8, azi), 0)

    def sweep(s, emit):
        def body(r, carry):
            base = pl.multiple_of(OWN + r * LINE, 8)
            above = pl.multiple_of(base + LINE + r // 3 * PAD, 8)
            x = [get(s, pl.ds(base + cf * 8, 8)) for cf in range(10)]
            for c in range(2):
                for g in range(5):
                    cf = 5 * c + g
                    mine = x[cf]
                    other = x[5 * (1 - c) + g]
                    turn = frequency * other
                    center = 6.0 * mine + mixes(g, x[5 * c : 5 * c + 5])
                    center = center - turn if c == 0 else center + turn
                    along = jnp.where(row == 7, 0.0, pltpu.roll(mine, 7, 0)) + jnp.where(
                        row == 0, 0.0, pltpu.roll(mine, 1, 0)
                    )
                    lines = get(s, pl.ds(base - LINE + cf * 8, 8)) + get(
                        s, pl.ds(above + cf * 8, 8)
                    )
                    after = jnp.where(last_lane, 0.0, pltpu.roll(mine, azi - 1, 1))
                    before = jnp.where(first_lane, 0.0, pltpu.roll(mine, 1, 1))
                    at = pl.multiple_of(r * LINE, 8) + cf * 8
                    image = center - (along + lines + (after + before))
                    emit(at, mine, get(source, pl.ds(at, 8)) - image)
            return carry

        lax.fori_loop(0, RD, body, 0)

    def add_inflow(strips, dst, first, scale):
        flow = scale * make_inflow(strips)
        last = dst.shape[0] - 1

        def body(r, carry):
            here = pltpu.roll(flow, 127 - 2 * r, 1)
            for cf in range(10):
                rows = pl.ds(pl.multiple_of(first + r * LINE, 8) + cf * 8, 8)
                ends = rolled(here, -cf * 8)
                dst[0, rows, :] = dst[0, rows, :] + jnp.where(lane8 == 0, ends, 0.0)
                dst[last, rows, :] = dst[last, rows, :] + jnp.where(lane8 == 127, ends, 0.0)
            return carry

        lax.fori_loop(0, RD, body, 0, unroll=True)

    def forward(s, out):
        halves = []
        for c in range(2):
            blocks = [
                get(s, pl.ds(OWN + r * LINE + c * 40 + 7 * x, 8, stride=8))
                for r in range(RD)
                for x in range(2)
            ]
            halves.append(jnp.concatenate(blocks, axis=0))
        re, im = ([h[:, a * quarter : (a + 1) * quarter] for a in range(4)] for h in halves)
        se, de, so, do = re[0] + re[2], re[0] - re[2], re[1] + re[3], re[1] - re[3]
        te, ue, to, uo = im[0] + im[2], im[0] - im[2], im[1] + im[3], im[1] - im[3]
        classes = [(se + so, te + to), (de + uo, ue - do), (se - so, te - to), (de - uo, ue + do)]
        modes = [None] * MODES
        for b, (yr, yi) in enumerate(classes):
            y = jnp.concatenate(
                [jnp.concatenate([yr, yi], axis=0), jnp.concatenate([yi, -yr], axis=0)], axis=1
            )
            z = dot3((ahead[0, b], ahead[1, b]), split(y), ((1,), (1,)))
            modes[b], modes[4 + b] = z[:n], z[n:]
        for f in range(5):
            part = rolled(modes[0], -f)
            for j in range(1, MODES):
                part = jnp.where(lane % 8 == j, rolled(modes[j], j - f), part)
            out[pl.ds(f, n, stride=8), :] = part

    def cycle_weight(g, f):
        return jnp.where(lane // 8 % 2 == 0, cycle_ref[g * 5 + f], cycle_ref[25 + g * 5 + f])

    block = lane // 16 % 4

    def filtered(modes):
        blended = []
        for g in range(5):
            total = cycle_weight(g, 0) * modes[0]
            for f in range(1, 5):
                total = total + cycle_weight(g, f) * modes[f]
            blended.append(total)
        for r in range(RD):
            part = rolled(blended[0], -16 * r)
            for g in range(1, 4):
                part = jnp.where(block == g, rolled(blended[g], 16 * (g - r)), part)
            packed[0, pl.ds(r, n, stride=RD), :] = part
            packed[1, pl.ds(r, n, stride=RD), :] = rolled(blended[4], -16 * r)
        x = jnp.concatenate([packed[0], packed[1]], axis=1)
        radial = dot3((basis_hi[...], basis_lo[...]), split(x))
        radial = radial * gain_rows[...]
        back_r = dot3((turned_hi[...], turned_lo[...]), split(radial))
        packed[0] = back_r[:, :128]
        packed[1] = back_r[:, 128:]
        lines0 = [packed[0, pl.ds(r, n, stride=RD), :] for r in range(RD)]
        lines1 = [packed[1, pl.ds(r, n, stride=RD), :] for r in range(RD)]
        result = []
        for g in range(5):
            lines, place = (lines0, g) if g < 4 else (lines1, 0)
            part = rolled(lines[0], -16 * place)
            for r in range(1, RD):
                part = jnp.where(block == r, rolled(lines[r], 16 * (r - place)), part)
            result.append(part)
        return result

    def inverse(modes):
        spread_modes = [modes[pl.ds(g, n, stride=8), :] for g in range(5)]
        z = []
        for j in range(MODES):
            part = rolled(spread_modes[0], -j)
            for g in range(1, 5):
                part = jnp.where(lane % 8 == g, rolled(spread_modes[g], g - j), part)
            z.append(part)
        v = []
        for b in range(4):
            turned = jnp.concatenate([z[b], z[4 + b]], axis=0).T
            y = jnp.concatenate(
                [turned, jnp.concatenate([-turned[64:], turned[:64]], axis=0)], axis=1
            )
            v.append(dot3(split(y), (back[0, b], back[1, b])))
        s, d, p, q = v[0] + v[2], v[0] - v[2], v[1] + v[3], v[1] - v[3]
        iq = jnp.concatenate([-q[64:], q[:64]], axis=0)
        points = jnp.concatenate([s + p, d + iq, s - p, d - iq], axis=1)
        for c in range(2):
            for r in range(RD):
                put(
                    ghosts,
                    pl.ds(r * 32 + c * 16, 16),
                    points[c * 64 + r * 16 : c * 64 + r * 16 + 16],
                )

    def add_ghosts(dst, first, values, start, scale):
        for c in range(2):
            for x in range(2):
                rows = pl.ds(first + c * 40 + 7 * x, 5, stride=8)
                ghost = get(values, pl.ds(start + c * 16 + x * 8, 8))[:5]
                put(dst, rows, get(dst, rows) + scale * ghost)

    seventh = 1.0 / 7.0
    loads[0].wait()
    spread(stage, s0, OWN)
    for s in (s0, s1):
        put(s, pl.ds(OWN + RD * LINE, PAD), jnp.zeros((PAD, azi), F32))

    @pl.when(me == 0)
    def _():
        for s in (s0, s1):
            put(s, pl.ds(0, LINE), jnp.zeros((LINE, azi), F32))

    @pl.when(me == n - 1)
    def _():
        for s in (s0, s1):
            put(s, pl.ds(UPPER, LINE), jnp.zeros((LINE, azi), F32))

    make_strip(s0, strips0)
    loads[1].wait()
    forward(s0, modes_out)
    loads[2].wait()
    spread(stage_source, source, 0)
    loads[3].wait()
    whole = basis[...]
    basis_hi[...], basis_lo[...] = split(whole)
    turned_hi[...], turned_lo[...] = split(whole.T)
    loads[4].wait()
    rows0 = [gain[x, g] for c in range(2) for g in range(4) for x in range(2)]
    rows1 = [gain[x, 4] for c in range(2) for g in range(4) for x in range(2)]
    gain_rows[:, :128] = jnp.concatenate(rows0, axis=0).T
    gain_rows[:, 128:] = jnp.concatenate(rows1, axis=0).T
    loads[5].wait()

    pl.semaphore_wait(barrier, n - 1)
    strip_z(0, strips0)
    halo0 = line_halo(0, s0)
    halo_start(halo0)
    exchange(0, modes_out, modes_in)
    strip_w(0, strips0)

    def emit_base(at, mine, value):
        put(s1, pl.ds(OWN + at, 8), mine + value * seventh)

    halo_recv_wait(halo0)
    sweep(s0, emit_base)

    exchange_wait(0, modes_in)
    first = filtered([modes_in[pl.ds(f, n, stride=8), :] for f in range(5)])
    for g in range(5):
        first_out[pl.ds(g, n, stride=8), :] = first[g]
    exchange(2, first_out, first_in)

    strip_wait(0, strips0)
    add_inflow(strips0, s1, OWN, seventh)
    forward(s1, late_out)
    exchange(1, late_out, late_in)

    exchange_wait(2, first_in)
    inverse(first_in)

    def own_ghosts(r, carry):
        add_ghosts(s1, OWN + r * LINE, ghosts, r * 32, seventh)
        return carry

    lax.fori_loop(0, RD, own_ghosts, 0, unroll=True)
    make_strip(s1, strips1)
    strip_z(1, strips1)
    halo1 = line_halo(1, s1)
    halo_start(halo1)

    exchange_wait(1, late_in)
    second = filtered(
        [
            late_in[pl.ds(f, n, stride=8), :] + seventh * first_out[pl.ds(f, n, stride=8), :]
            for f in range(5)
        ]
    )
    for g in range(5):
        second_out[pl.ds(g, n, stride=8), :] = second[g]
    exchange(3, second_out, second_in)
    strip_w(1, strips1)

    def emit_residual(at, mine, value):
        put(res, pl.ds(at, 8), value)

    halo_recv_wait(halo1)
    sweep(s1, emit_residual)
    strip_wait(1, strips1)
    add_inflow(strips1, res, 0, 1.0)

    def relax(i, carry):
        at = pl.multiple_of(i * 16, 8)
        rows = pl.ds(at, 16)
        put(source, rows, get(s1, pl.ds(OWN + at, 16)) + get(res, rows) * seventh)
        return carry

    lax.fori_loop(0, RD * LINE // 16, relax, 0, unroll=4)
    writes = []

    def write(i, staged, out, first_station, count):
        part = (slice(None), pl.ds(first_station, count))
        copy = pltpu.make_async_copy(staged.at[part], out.at[part], load_sem.at[i])
        copy.start()
        writes.append(copy)

    middle = range(1, AX - 1)
    collect(res, stage_source, middle)
    write(0, stage_source, residual_hbm, 1, AX - 2)
    collect(source, stage, middle)
    write(1, stage, relaxed_hbm, 1, AX - 2)

    exchange_wait(3, second_in)
    inverse(second_in)

    def last_ghosts(r, carry):
        add_ghosts(res, r * LINE, ghosts, r * 32, 1.0)
        add_ghosts(source, r * LINE, ghosts, r * 32, seventh)
        return carry

    lax.fori_loop(0, RD, last_ghosts, 0, unroll=True)
    ends = (0, AX - 1)
    collect(res, stage_source, ends)
    collect(source, stage, ends)
    for place, station in enumerate(ends):
        write(2 + place, stage_source, residual_hbm, station, 1)
        write(4 + place, stage, relaxed_hbm, station, 1)

    for i, out in enumerate((modes_out, late_out, first_out, second_out)):
        arrived(all_send.at[i], out.at[pl.ds(0, (n - 1) * 5)])
    for i, strips in enumerate((strips0, strips1)):
        arrived(group_sent.at[2 * i], strips.at[pl.ds(0, (nz - 1) * 8)])
        arrived(group_sent.at[2 * i + 1], strips.at[pl.ds(0, (wide - 1) * nz * 8)])
    halo_send_wait(halo0)
    halo_send_wait(halo1)
    for copy in writes:
        copy.wait()


def on_device(
    n,
    initial_state,
    source,
    field_coupling,
    frequency,
    phase_angle,
    face_owner,
    face_slot,
    radial_basis,
    cycle_coupling,
    cycle_gain,
):
    azi = MODES * n
    rad = RD * n
    quarter = azi // 4
    ahead, back = fourier_tables(n)
    shape = (10, AX, RD, azi)
    hbm = pl.BlockSpec(memory_space=pl.ANY)
    smem = pl.BlockSpec(memory_space=pltpu.SMEM)
    vmem = pltpu.VMEM
    peers = (n * 8, 128)
    return pl.pallas_call(
        functools.partial(kernel, n, 8 if n >= 64 else 4),
        out_shape=(jax.ShapeDtypeStruct(shape, F32), jax.ShapeDtypeStruct(shape, F32)),
        in_specs=[hbm] * 6 + [smem] * 6,
        out_specs=(hbm, hbm),
        scratch_shapes=[
            vmem(shape, F32),
            vmem(shape, F32),
            vmem((2, 5, MODES, rad), F32),
            vmem((rad, rad), F32),
            vmem((2, 4, quarter, 2 * quarter), BF16),
            vmem((2, 4, 2 * quarter, quarter), BF16),
            vmem((azi // 128, ROWS, 128), F32),
            vmem((azi // 128, ROWS, 128), F32),
            vmem((azi // 128, RD * LINE, 128), F32),
            vmem((azi // 128, RD * LINE, 128), F32),
            vmem((rad, rad), BF16),
            vmem((rad, rad), BF16),
            vmem((rad, rad), BF16),
            vmem((rad, rad), BF16),
            vmem((rad, 256), F32),
            vmem(peers, F32),
            vmem(peers, F32),
            *[vmem(peers, F32) for _ in range(8)],
            vmem((2, rad, 128), F32),
            vmem((azi // 128, RD * 32, 128), F32),
            pltpu.SemaphoreType.DMA((6,)),
            pltpu.SemaphoreType.DMA((4,)),
            pltpu.SemaphoreType.DMA((4,)),
            pltpu.SemaphoreType.DMA((4,)),
            pltpu.SemaphoreType.DMA((4,)),
            pltpu.SemaphoreType.DMA((4,)),
            pltpu.SemaphoreType.DMA((4,)),
        ],
        compiler_params=pltpu.CompilerParams(
            collective_id=0, has_side_effects=True, vmem_limit_bytes=62 * 1024 * 1024
        ),
    )(
        initial_state,
        source,
        jnp.transpose(cycle_gain, (0, 1, 3, 2)),
        radial_basis,
        jnp.asarray(ahead),
        jnp.asarray(back),
        field_coupling,
        frequency,
        phase_angle,
        face_owner.reshape(-1),
        face_slot,
        cycle_coupling.reshape(-1),
    )


def solution(mesh):
    P = jax.sharding.PartitionSpec
    state = P("ibpa", None, "dom", None)
    in_specs = (
        state,
        state,
        P(),
        P(),
        P("ibpa"),
        P("dom", None),
        P("dom"),
        P(),
        P(),
        P(None, None, None, "dom"),
    )
    return jax.shard_map(
        functools.partial(on_device, mesh.shape["dom"]),
        mesh=mesh,
        in_specs=in_specs,
        out_specs=(state, state),
        check_vma=False,
    )
```

```python
import functools

import jax
import jax.numpy as jnp
import ml_dtypes
import numpy as np
from jax import lax
from jax.experimental import pallas as pl
from jax.experimental.pallas import tpu as pltpu

F32 = jnp.float32
BF16 = jnp.bfloat16
AX = 8
RD = 4
MODES = 8
LINE = 80
OWN = LINE
PAD = 24
UPPER = OWN + RD * LINE + PAD
ROWS = UPPER + LINE
MESH = pl.DeviceIdType.MESH


@functools.lru_cache(None)
def fourier_tables(count):
    azi = MODES * count
    quarter = azi // 4
    kk, e = np.arange(quarter) // count, np.arange(quarter) % count
    k = 2 * e + kk
    t = np.arange(quarter)
    ahead, back = [], []
    for b in range(4):
        angle = ((4 * k + b)[:, None] * t[None, :]) % azi * (2 * np.pi / azi)
        ahead.append(np.concatenate([np.cos(angle), np.sin(angle)], axis=1))
        back.append(np.concatenate([np.cos(angle), np.sin(angle)], axis=0) / azi)

    def split(x):
        x = x.astype(np.float32)
        hi = x.astype(ml_dtypes.bfloat16)
        lo = (x - hi.astype(np.float32)).astype(ml_dtypes.bfloat16)
        return np.stack([hi, lo])

    return split(np.stack(ahead)), split(np.stack(back))


def split(x):
    hi = x.astype(BF16)
    return hi, (x - hi.astype(F32)).astype(BF16)


def dot3(a, b, contract=((1,), (0,))):
    dims = (contract, ((), ()))

    def one(u, v):
        return lax.dot_general(u, v, dims, preferred_element_type=F32)

    return one(a[0], b[0]) + (one(a[1], b[0]) + one(a[0], b[1]))


def get(ref, rows):
    return jnp.concatenate([ref[tile, rows, :] for tile in range(ref.shape[0])], axis=1)


def put(ref, rows, value):
    for tile in range(ref.shape[0]):
        ref[tile, rows, :] = value[:, tile * 128 : (tile + 1) * 128]


def rolled(x, shift):
    shift = shift % 128
    return x if shift == 0 else pltpu.roll(x, shift, 1)


def kernel(
    n,
    wide,
    state_hbm,
    source_hbm,
    gain_hbm,
    basis_hbm,
    ahead_hbm,
    back_hbm,
    mix_ref,
    frequency_ref,
    phase_ref,
    owner_ref,
    slot_ref,
    cycle_ref,
    relaxed,
    residual,
    stage,
    stage_source,
    gain,
    basis,
    ahead,
    back,
    s0,
    s1,
    source,
    res,
    basis_hi,
    basis_lo,
    turned_hi,
    turned_lo,
    gain_rows,
    strips0,
    strips1,
    modes_out,
    modes_in,
    late_out,
    late_in,
    first_out,
    first_in,
    second_out,
    second_in,
    packed,
    ghosts,
    load_sem,
    all_send,
    all_recv,
    group_sent,
    group_recv,
    halo_send,
    halo_recv,
):
    azi = MODES * n
    quarter = azi // 4
    rad = RD * n
    nz = n // wide
    me = lax.axis_index("dom")
    my_z, my_w = me // wide, me % wide
    barrier = pltpu.get_barrier_semaphore()

    lane = lax.broadcasted_iota(jnp.int32, (1, 128), 1)
    row8 = lax.broadcasted_iota(jnp.int32, (8, 128), 0)
    lane8 = lax.broadcasted_iota(jnp.int32, (8, 128), 1)

    def peer_of(i):
        return (me + n // 2 + (i % 2) * ((i + 1) // 2) - (1 - i % 2) * (i // 2)) % n

    def greet(step, carry):
        pl.semaphore_signal(
            barrier, inc=1, device_id={"dom": peer_of(step)}, device_id_type=MESH
        )
        return carry

    lax.fori_loop(0, n - 1, greet, 0)

    def load(i, src, dst):
        return pltpu.make_async_copy(src, dst, load_sem.at[i])

    loads = [
        load(0, state_hbm, stage),
        load(1, ahead_hbm, ahead),
        load(2, source_hbm, stage_source),
        load(3, basis_hbm, basis),
        load(4, gain_hbm, gain),
        load(5, back_hbm, back),
    ]
    for copy in loads:
        copy.start()

    def send_all(i, src_of, dst):
        def send(step, carry):
            peer = peer_of(step)
            pltpu.make_async_remote_copy(
                src_ref=src_of(peer),
                dst_ref=dst,
                send_sem=all_send.at[i],
                recv_sem=all_recv.at[i],
                device_id={"dom": peer},
                device_id_type=MESH,
            ).start()
            return carry

        lax.fori_loop(0, n - 1, send, 0, unroll=True)

    def tile_rows(device, count):
        return pl.ds(pl.multiple_of(device * 8, 8), count)

    def exchange(i, out, into):
        send_all(i, lambda peer: out.at[tile_rows(peer, 5)], into.at[tile_rows(me, 5)])
        into[tile_rows(me, 8), :] = out[tile_rows(me, 8), :]

    def arrived(sem, ref):
        pltpu.make_async_copy(ref, ref, sem).wait()

    def exchange_wait(i, into):
        arrived(all_recv.at[i], into.at[pl.ds(0, (n - 1) * 5)])

    def group_send(i, count, peer_at, block):
        def send(step, carry):
            pltpu.make_async_remote_copy(
                src_ref=block,
                dst_ref=block,
                send_sem=group_sent.at[i],
                recv_sem=group_recv.at[i],
                device_id={"dom": peer_at(step)},
                device_id_type=MESH,
            ).start()
            return carry

        lax.fori_loop(1, count, send, 0, unroll=True)

    my_tile = my_w * nz + my_z

    def strip_z(i, strips):
        block = strips.at[pl.ds(my_tile, 1), pl.ds(0, 5)]
        group_send(2 * i, nz, lambda step: (my_z + step) % nz * wide + my_w, block)

    def strip_w(i, strips):
        arrived(group_recv.at[2 * i], strips.at[pl.ds(0, nz - 1), pl.ds(0, 5)])
        block = strips.at[pl.ds(my_w * nz, nz), pl.ds(0, 5)]
        group_send(2 * i + 1, wide, lambda step: my_z * wide + (my_w + step) % wide, block)

    def strip_wait(i, strips):
        arrived(group_recv.at[2 * i + 1], strips.at[pl.ds(0, (wide - 1) * nz), pl.ds(0, 5)])

    def halo_copies(i, low_src, low_dst, up_src, up_dst):
        down = pltpu.make_async_remote_copy(
            src_ref=low_src,
            dst_ref=up_dst,
            send_sem=halo_send.at[2 * i],
            recv_sem=halo_recv.at[2 * i],
            device_id={"dom": jnp.maximum(me - 1, 0)},
            device_id_type=MESH,
        )
        up = pltpu.make_async_remote_copy(
            src_ref=up_src,
            dst_ref=low_dst,
            send_sem=halo_send.at[2 * i + 1],
            recv_sem=halo_recv.at[2 * i + 1],
            device_id={"dom": jnp.minimum(me + 1, n - 1)},
            device_id_type=MESH,
        )
        return down, up

    def halo_start(copies):
        @pl.when(me > 0)
        def _():
            copies[0].start()

        @pl.when(me < n - 1)
        def _():
            copies[1].start()

    def halo_recv_wait(copies):
        @pl.when(me < n - 1)
        def _():
            copies[0].wait_recv()

        @pl.when(me > 0)
        def _():
            copies[1].wait_recv()

    def halo_send_wait(copies):
        @pl.when(me > 0)
        def _():
            copies[0].wait_send()

        @pl.when(me < n - 1)
        def _():
            copies[1].wait_send()

    def line_halo(i, s):
        return halo_copies(
            i,
            s.at[:, pl.ds(OWN, LINE)],
            s.at[:, pl.ds(0, LINE)],
            s.at[:, pl.ds(OWN + 3 * LINE, LINE)],
            s.at[:, pl.ds(UPPER, LINE)],
        )

    def spread(staged, dst, first):
        def body(cf, carry):
            for a in range(AX):
                put(dst, pl.ds(first + cf * 8 + a, RD, stride=LINE), staged[cf, a])
            return carry

        lax.fori_loop(0, 10, body, 0)

    def collect(src, staged, stations):
        def body(cf, carry):
            for a in stations:
                staged[cf, a] = get(src, pl.ds(cf * 8 + a, RD, stride=LINE))
            return carry

        lax.fori_loop(0, 10, body, 0)

    group8 = lane8 // 8 % 8

    def by_field(x):
        turned = jnp.zeros((8, 128), F32)
        for delta in range(-7, 8):
            moved = x if delta == 0 else pltpu.roll(rolled(x, 8 * delta), -delta % 8, 0)
            turned = jnp.where(group8 - row8 == delta, moved, turned)
        return turned

    def make_strip(s, strips):
        def body(r, acc):
            base = pl.multiple_of(OWN + r * LINE, 8)
            part = jnp.zeros((8, 128), F32)
            for cf in range(10):
                ends = jnp.where(
                    lane8 == 0,
                    s[0, pl.ds(base + cf * 8, 8), :],
                    s[s.shape[0] - 1, pl.ds(base + cf * 8, 8), :],
                )
                part = jnp.where(lane8 // 2 == cf * 4, rolled(ends, cf * 8 + 1), part)
            part = pltpu.roll(part, 2 * r, 1)
            return jnp.where(lane8 % 8 // 2 == r, part, acc)

        tile = lax.fori_loop(0, RD, body, jnp.zeros((8, 128), F32), unroll=True)
        strips[my_tile] = by_field(jnp.where(lane8 < 40, tile, rolled(tile, 24)))

    angle = jnp.broadcast_to(phase_ref[0], (8, 128))
    cos_value, sin_value = jnp.cos(angle), jnp.sin(angle)

    def make_inflow(strips):
        def body(a, acc):
            for side in range(2):
                for r in range(RD):
                    face = side * AX * RD + a * RD + r
                    owner = owner_ref[face]
                    slot = slot_ref[face]
                    entry = strips[owner % wide * nz + owner // wide]
                    to = a * 8 + 2 * r + 1 - side
                    moved = pltpu.roll(entry, to - (slot * 2 + side) + 128, 1)
                    acc = jnp.where(lane8 % 64 == to, moved, acc)
            return acc

        partner = lax.fori_loop(0, AX, body, jnp.zeros((8, 128), F32), unroll=True)
        other = rolled(partner, 64)
        plus = (lane8 < 64) == (lane8 % 2 == 1)
        flow = cos_value * partner + jnp.where(plus, sin_value, -sin_value) * other
        flow = by_field(flow)
        return jnp.where(lane8 < 40, flow, rolled(flow, -24))

    def mixes(g, x):
        total = mix_ref[g, 0] * x[0]
        for f in range(1, 5):
            total = total + mix_ref[g, f] * x[f]
        return total

    frequency = frequency_ref[0]
    first_lane = lax.broadcasted_iota(jnp.int32, (8, azi), 1) == 0
    last_lane = lax.broadcasted_iota(jnp.int32, (8, azi), 1) == azi - 1
    row = lax.broadcasted_iota(jnp.int32, (8, azi), 0)

    def sweep(s, emit):
        def body(r, carry):
            base = pl.multiple_of(OWN + r * LINE, 8)
            above = pl.multiple_of(base + LINE + r // 3 * PAD, 8)
            x = [get(s, pl.ds(base + cf * 8, 8)) for cf in range(10)]
            for c in range(2):
                for g in range(5):
                    cf = 5 * c + g
                    mine = x[cf]
                    other = x[5 * (1 - c) + g]
                    turn = frequency * other
                    center = 6.0 * mine + mixes(g, x[5 * c : 5 * c + 5])
                    center = center - turn if c == 0 else center + turn
                    along = jnp.where(row == 7, 0.0, pltpu.roll(mine, 7, 0)) + jnp.where(
                        row == 0, 0.0, pltpu.roll(mine, 1, 0)
                    )
                    lines = get(s, pl.ds(base - LINE + cf * 8, 8)) + get(
                        s, pl.ds(above + cf * 8, 8)
                    )
                    after = jnp.where(last_lane, 0.0, pltpu.roll(mine, azi - 1, 1))
                    before = jnp.where(first_lane, 0.0, pltpu.roll(mine, 1, 1))
                    at = pl.multiple_of(r * LINE, 8) + cf * 8
                    image = center - (along + lines + (after + before))
                    emit(at, mine, get(source, pl.ds(at, 8)) - image)
            return carry

        lax.fori_loop(0, RD, body, 0)

    def add_inflow(strips, dst, first, scale):
        flow = scale * make_inflow(strips)
        last = dst.shape[0] - 1

        def body(r, carry):
            here = pltpu.roll(flow, 127 - 2 * r, 1)
            for cf in range(10):
                rows = pl.ds(pl.multiple_of(first + r * LINE, 8) + cf * 8, 8)
                ends = rolled(here, -cf * 8)
                dst[0, rows, :] = dst[0, rows, :] + jnp.where(lane8 == 0, ends, 0.0)
                dst[last, rows, :] = dst[last, rows, :] + jnp.where(lane8 == 127, ends, 0.0)
            return carry

        lax.fori_loop(0, RD, body, 0, unroll=True)

    def forward(s, out):
        halves = []
        for c in range(2):
            blocks = [
                get(s, pl.ds(OWN + r * LINE + c * 40 + 7 * x, 8, stride=8))
                for r in range(RD)
                for x in range(2)
            ]
            halves.append(jnp.concatenate(blocks, axis=0))
        re, im = ([h[:, a * quarter : (a + 1) * quarter] for a in range(4)] for h in halves)
        se, de, so, do = re[0] + re[2], re[0] - re[2], re[1] + re[3], re[1] - re[3]
        te, ue, to, uo = im[0] + im[2], im[0] - im[2], im[1] + im[3], im[1] - im[3]
        classes = [(se + so, te + to), (de + uo, ue - do), (se - so, te - to), (de - uo, ue + do)]
        modes = [None] * MODES
        for b, (yr, yi) in enumerate(classes):
            y = jnp.concatenate(
                [jnp.concatenate([yr, yi], axis=0), jnp.concatenate([yi, -yr], axis=0)], axis=1
            )
            z = dot3((ahead[0, b], ahead[1, b]), split(y), ((1,), (1,)))
            modes[b], modes[4 + b] = z[:n], z[n:]
        for f in range(5):
            part = rolled(modes[0], -f)
            for j in range(1, MODES):
                part = jnp.where(lane % 8 == j, rolled(modes[j], j - f), part)
            out[pl.ds(f, n, stride=8), :] = part

    def cycle_weight(g, f):
        return jnp.where(lane // 8 % 2 == 0, cycle_ref[g, 0, f], cycle_ref[g, 1, f])

    block = lane // 16 % 4

    def filtered(modes):
        blended = []
        for g in range(5):
            total = cycle_weight(g, 0) * modes[0]
            for f in range(1, 5):
                total = total + cycle_weight(g, f) * modes[f]
            blended.append(total)
        for r in range(RD):
            part = rolled(blended[0], -16 * r)
            for g in range(1, 4):
                part = jnp.where(block == g, rolled(blended[g], 16 * (g - r)), part)
            packed[0, pl.ds(r, n, stride=RD), :] = part
            packed[1, pl.ds(r, n, stride=RD), :] = rolled(blended[4], -16 * r)
        x = jnp.concatenate([packed[0], packed[1]], axis=1)
        radial = dot3((basis_hi[...], basis_lo[...]), split(x))
        radial = radial * gain_rows[...]
        back_r = dot3((turned_hi[...], turned_lo[...]), split(radial))
        packed[0] = back_r[:, :128]
        packed[1] = back_r[:, 128:]
        lines0 = [packed[0, pl.ds(r, n, stride=RD), :] for r in range(RD)]
        lines1 = [packed[1, pl.ds(r, n, stride=RD), :] for r in range(RD)]
        result = []
        for g in range(5):
            lines, place = (lines0, g) if g < 4 else (lines1, 0)
            part = rolled(lines[0], -16 * place)
            for r in range(1, RD):
                part = jnp.where(block == r, rolled(lines[r], 16 * (r - place)), part)
            result.append(part)
        return result

    def inverse(modes):
        spread_modes = [modes[pl.ds(g, n, stride=8), :] for g in range(5)]
        z = []
        for j in range(MODES):
            part = rolled(spread_modes[0], -j)
            for g in range(1, 5):
                part = jnp.where(lane % 8 == g, rolled(spread_modes[g], g - j), part)
            z.append(part)
        v = []
        for b in range(4):
            turned = jnp.concatenate([z[b], z[4 + b]], axis=0).T
            y = jnp.concatenate(
                [turned, jnp.concatenate([-turned[64:], turned[:64]], axis=0)], axis=1
            )
            v.append(dot3(split(y), (back[0, b], back[1, b])))
        s, d, p, q = v[0] + v[2], v[0] - v[2], v[1] + v[3], v[1] - v[3]
        iq = jnp.concatenate([-q[64:], q[:64]], axis=0)
        points = jnp.concatenate([s + p, d + iq, s - p, d - iq], axis=1)
        for c in range(2):
            for r in range(RD):
                put(
                    ghosts,
                    pl.ds(r * 32 + c * 16, 16),
                    points[c * 64 + r * 16 : c * 64 + r * 16 + 16],
                )

    def add_ghosts(dst, first, values, start, scale):
        for c in range(2):
            for x in range(2):
                rows = pl.ds(first + c * 40 + 7 * x, 5, stride=8)
                ghost = get(values, pl.ds(start + c * 16 + x * 8, 8))[:5]
                put(dst, rows, get(dst, rows) + scale * ghost)

    seventh = 1.0 / 7.0
    loads[0].wait()
    spread(stage, s0, OWN)
    for s in (s0, s1):
        put(s, pl.ds(OWN + RD * LINE, PAD), jnp.zeros((PAD, azi), F32))

    @pl.when(me == 0)
    def _():
        for s in (s0, s1):
            put(s, pl.ds(0, LINE), jnp.zeros((LINE, azi), F32))

    @pl.when(me == n - 1)
    def _():
        for s in (s0, s1):
            put(s, pl.ds(UPPER, LINE), jnp.zeros((LINE, azi), F32))

    make_strip(s0, strips0)
    loads[1].wait()
    forward(s0, modes_out)
    loads[2].wait()
    spread(stage_source, source, 0)
    loads[3].wait()
    whole = basis[...]
    basis_hi[...], basis_lo[...] = split(whole)
    turned_hi[...], turned_lo[...] = split(whole.T)
    loads[4].wait()
    rows0 = [gain[x, g] for c in range(2) for g in range(4) for x in range(2)]
    rows1 = [gain[x, 4] for c in range(2) for g in range(4) for x in range(2)]
    gain_rows[:, :128] = jnp.concatenate(rows0, axis=0).T
    gain_rows[:, 128:] = jnp.concatenate(rows1, axis=0).T
    loads[5].wait()

    pl.semaphore_wait(barrier, n - 1)
    strip_z(0, strips0)
    halo0 = line_halo(0, s0)
    halo_start(halo0)
    exchange(0, modes_out, modes_in)
    strip_w(0, strips0)

    def emit_base(at, mine, value):
        put(s1, pl.ds(OWN + at, 8), mine + value * seventh)

    halo_recv_wait(halo0)
    sweep(s0, emit_base)

    exchange_wait(0, modes_in)
    first = filtered([modes_in[pl.ds(f, n, stride=8), :] for f in range(5)])
    for g in range(5):
        first_out[pl.ds(g, n, stride=8), :] = first[g]
    exchange(2, first_out, first_in)

    strip_wait(0, strips0)
    add_inflow(strips0, s1, OWN, seventh)
    forward(s1, late_out)
    exchange(1, late_out, late_in)

    exchange_wait(2, first_in)
    inverse(first_in)

    def own_ghosts(r, carry):
        add_ghosts(s1, OWN + r * LINE, ghosts, r * 32, seventh)
        return carry

    lax.fori_loop(0, RD, own_ghosts, 0, unroll=True)
    make_strip(s1, strips1)
    strip_z(1, strips1)
    halo1 = line_halo(1, s1)
    halo_start(halo1)

    exchange_wait(1, late_in)
    second = filtered(
        [
            late_in[pl.ds(f, n, stride=8), :] + seventh * first_out[pl.ds(f, n, stride=8), :]
            for f in range(5)
        ]
    )
    for g in range(5):
        second_out[pl.ds(g, n, stride=8), :] = second[g]
    exchange(3, second_out, second_in)
    strip_w(1, strips1)

    def emit_residual(at, mine, value):
        put(res, pl.ds(at, 8), value)

    halo_recv_wait(halo1)
    sweep(s1, emit_residual)
    strip_wait(1, strips1)
    add_inflow(strips1, res, 0, 1.0)

    def relax(i, carry):
        at = pl.multiple_of(i * 16, 8)
        rows = pl.ds(at, 16)
        put(source, rows, get(s1, pl.ds(OWN + at, 16)) + get(res, rows) * seventh)
        return carry

    lax.fori_loop(0, RD * LINE // 16, relax, 0, unroll=4)
    middle = range(1, AX - 1)
    collect(res, residual, middle)
    collect(source, relaxed, middle)

    exchange_wait(3, second_in)
    inverse(second_in)

    def last_ghosts(r, carry):
        add_ghosts(res, r * LINE, ghosts, r * 32, 1.0)
        add_ghosts(source, r * LINE, ghosts, r * 32, seventh)
        return carry

    lax.fori_loop(0, RD, last_ghosts, 0, unroll=True)
    ends = (0, AX - 1)
    collect(res, residual, ends)
    collect(source, relaxed, ends)

    for i, out in enumerate((modes_out, late_out, first_out, second_out)):
        arrived(all_send.at[i], out.at[pl.ds(0, (n - 1) * 5)])
    for i, strips in enumerate((strips0, strips1)):
        arrived(group_sent.at[2 * i], strips.at[pl.ds(0, nz - 1), pl.ds(0, 5)])
        arrived(group_sent.at[2 * i + 1], strips.at[pl.ds(0, (wide - 1) * nz), pl.ds(0, 5)])
    halo_send_wait(halo0)
    halo_send_wait(halo1)


def write_kernel(relaxed, residual, relaxed_hbm, residual_hbm, sem):
    copies = [
        pltpu.make_async_copy(relaxed, relaxed_hbm, sem.at[0]),
        pltpu.make_async_copy(residual, residual_hbm, sem.at[1]),
    ]
    for copy in copies:
        copy.start()
    for copy in copies:
        copy.wait()


def on_device(
    n,
    initial_state,
    source,
    field_coupling,
    frequency,
    phase_angle,
    face_owner,
    face_slot,
    radial_basis,
    cycle_coupling,
    cycle_gain,
):
    azi = MODES * n
    rad = RD * n
    quarter = azi // 4
    ahead, back = fourier_tables(n)
    shape = (10, AX, RD, azi)
    hbm = pl.BlockSpec(memory_space=pl.ANY)
    smem = pl.BlockSpec(memory_space=pltpu.SMEM)
    vmem = pltpu.VMEM
    peers = (n * 8, 128)
    relaxed, residual = pl.pallas_call(
        functools.partial(kernel, n, 8 if n >= 64 else 4),
        out_shape=(vmem(shape, F32), vmem(shape, F32)),
        in_specs=[hbm] * 6 + [smem] * 6,
        out_specs=(pl.BlockSpec(memory_space=vmem), pl.BlockSpec(memory_space=vmem)),
        scratch_shapes=[
            vmem(shape, F32),
            vmem(shape, F32),
            vmem((2, 5, MODES, rad), F32),
            vmem((rad, rad), F32),
            vmem((2, 4, quarter, 2 * quarter), BF16),
            vmem((2, 4, 2 * quarter, quarter), BF16),
            vmem((azi // 128, ROWS, 128), F32),
            vmem((azi // 128, ROWS, 128), F32),
            vmem((azi // 128, RD * LINE, 128), F32),
            vmem((azi // 128, RD * LINE, 128), F32),
            vmem((rad, rad), BF16),
            vmem((rad, rad), BF16),
            vmem((rad, rad), BF16),
            vmem((rad, rad), BF16),
            vmem((rad, 256), F32),
            vmem((n, 8, 128), F32),
            vmem((n, 8, 128), F32),
            *[vmem(peers, F32) for _ in range(8)],
            vmem((2, rad, 128), F32),
            vmem((azi // 128, RD * 32, 128), F32),
            pltpu.SemaphoreType.DMA((6,)),
            pltpu.SemaphoreType.DMA((4,)),
            pltpu.SemaphoreType.DMA((4,)),
            pltpu.SemaphoreType.DMA((4,)),
            pltpu.SemaphoreType.DMA((4,)),
            pltpu.SemaphoreType.DMA((4,)),
            pltpu.SemaphoreType.DMA((4,)),
        ],
        compiler_params=pltpu.CompilerParams(
            collective_id=0, has_side_effects=True, vmem_limit_bytes=62 * 1024 * 1024
        ),
    )(
        initial_state,
        source,
        jnp.transpose(cycle_gain, (0, 1, 3, 2)),
        radial_basis,
        jnp.asarray(ahead),
        jnp.asarray(back),
        field_coupling,
        frequency,
        phase_angle,
        face_owner.reshape(-1),
        face_slot,
        jnp.transpose(cycle_coupling, (1, 0, 2)),
    )
    return pl.pallas_call(
        write_kernel,
        out_shape=(jax.ShapeDtypeStruct(shape, F32), jax.ShapeDtypeStruct(shape, F32)),
        in_specs=[hbm, hbm],
        out_specs=(hbm, hbm),
        scratch_shapes=[pltpu.SemaphoreType.DMA((2,))],
        compiler_params=pltpu.CompilerParams(vmem_limit_bytes=4 * 1024 * 1024),
    )(relaxed, residual)


def solution(mesh):
    P = jax.sharding.PartitionSpec
    state = P("ibpa", None, "dom", None)
    in_specs = (
        state,
        state,
        P(),
        P(),
        P("ibpa"),
        P("dom", None),
        P("dom"),
        P(),
        P(),
        P(None, None, None, "dom"),
    )
    return jax.shard_map(
        functools.partial(on_device, mesh.shape["dom"]),
        mesh=mesh,
        in_specs=in_specs,
        out_specs=(state, state),
        check_vma=False,
    )
```

```python
import functools

import jax
import jax.numpy as jnp
import ml_dtypes
import numpy as np
from jax import lax
from jax.experimental import pallas as pl
from jax.experimental.pallas import tpu as pltpu

F32 = jnp.float32
BF16 = jnp.bfloat16
AX = 8
RD = 4
MODES = 8
LINE = 80
OWN = LINE
PAD = 24
UPPER = OWN + RD * LINE + PAD
ROWS = UPPER + LINE
MESH = pl.DeviceIdType.MESH


@functools.lru_cache(None)
def fourier_tables(count):
    azi = MODES * count
    quarter = azi // 4
    kk, e = np.arange(quarter) // count, np.arange(quarter) % count
    k = 2 * e + kk
    t = np.arange(quarter)
    ahead, back = [], []
    for b in range(4):
        angle = ((4 * k + b)[:, None] * t[None, :]) % azi * (2 * np.pi / azi)
        ahead.append(np.concatenate([np.cos(angle), np.sin(angle)], axis=1))
        back.append(np.concatenate([np.cos(angle), np.sin(angle)], axis=0) / azi)

    def split(x):
        x = x.astype(np.float32)
        hi = x.astype(ml_dtypes.bfloat16)
        lo = (x - hi.astype(np.float32)).astype(ml_dtypes.bfloat16)
        return np.stack([hi, lo])

    return split(np.stack(ahead)), split(np.stack(back))


def split(x):
    hi = x.astype(BF16)
    return hi, (x - hi.astype(F32)).astype(BF16)


def dot3(a, b, contract=((1,), (0,))):
    dims = (contract, ((), ()))

    def one(u, v):
        return lax.dot_general(u, v, dims, preferred_element_type=F32)

    return one(a[0], b[0]) + (one(a[1], b[0]) + one(a[0], b[1]))


def get(ref, rows):
    return jnp.concatenate([ref[tile, rows, :] for tile in range(ref.shape[0])], axis=1)


def put(ref, rows, value):
    for tile in range(ref.shape[0]):
        ref[tile, rows, :] = value[:, tile * 128 : (tile + 1) * 128]


def rolled(x, shift):
    shift = shift % 128
    return x if shift == 0 else pltpu.roll(x, shift, 1)


def kernel(
    n,
    wide,
    state_hbm,
    source_hbm,
    gain_hbm,
    basis_hbm,
    ahead_hbm,
    back_hbm,
    mix_ref,
    frequency_ref,
    phase_ref,
    owner_ref,
    slot_ref,
    cycle_ref,
    relaxed,
    residual,
    stage,
    stage_source,
    gain,
    basis,
    ahead,
    back,
    s0,
    s1,
    source,
    res,
    basis_hi,
    basis_lo,
    turned_hi,
    turned_lo,
    gain_rows,
    strips0,
    strips1,
    modes_out,
    modes_in,
    late_out,
    late_in,
    first_out,
    first_in,
    second_out,
    second_in,
    packed,
    ghosts,
    face_tile,
    face_shift,
    load_sem,
    all_send,
    all_recv,
    group_sent,
    group_recv,
    halo_send,
    halo_recv,
):
    azi = MODES * n
    quarter = azi // 4
    rad = RD * n
    nz = n // wide
    me = lax.axis_index("dom")
    my_z, my_w = me // wide, me % wide
    barrier = pltpu.get_barrier_semaphore()

    lane = lax.broadcasted_iota(jnp.int32, (1, 128), 1)
    row8 = lax.broadcasted_iota(jnp.int32, (8, 128), 0)
    lane8 = lax.broadcasted_iota(jnp.int32, (8, 128), 1)

    def peer_of(i):
        return (me + n // 2 + (i % 2) * ((i + 1) // 2) - (1 - i % 2) * (i // 2)) % n

    def greet(step, carry):
        pl.semaphore_signal(
            barrier, inc=1, device_id={"dom": peer_of(step)}, device_id_type=MESH
        )
        return carry

    lax.fori_loop(0, n - 1, greet, 0, unroll=True)

    def load(i, src, dst):
        return pltpu.make_async_copy(src, dst, load_sem.at[i])

    loads = [
        load(0, state_hbm, stage),
        load(1, ahead_hbm, ahead),
        load(2, source_hbm, stage_source),
        load(3, basis_hbm, basis),
        load(4, gain_hbm, gain),
        load(5, back_hbm, back),
    ]
    for copy in loads:
        copy.start()

    def send_all(i, src_of, dst):
        def send(step, carry):
            peer = peer_of(step)
            pltpu.make_async_remote_copy(
                src_ref=src_of(peer),
                dst_ref=dst,
                send_sem=all_send.at[i],
                recv_sem=all_recv.at[i],
                device_id={"dom": peer},
                device_id_type=MESH,
            ).start()
            return carry

        lax.fori_loop(0, n - 1, send, 0, unroll=True)

    def tile_rows(device, count):
        return pl.ds(pl.multiple_of(device * 8, 8), count)

    def exchange(i, out, into):
        send_all(i, lambda peer: out.at[tile_rows(peer, 5)], into.at[tile_rows(me, 5)])
        into[tile_rows(me, 8), :] = out[tile_rows(me, 8), :]

    def arrived(sem, ref):
        pltpu.make_async_copy(ref, ref, sem).wait()

    def exchange_wait(i, into):
        arrived(all_recv.at[i], into.at[pl.ds(0, (n - 1) * 5)])

    def group_send(i, count, peer_at, block):
        def send(step, carry):
            pltpu.make_async_remote_copy(
                src_ref=block,
                dst_ref=block,
                send_sem=group_sent.at[i],
                recv_sem=group_recv.at[i],
                device_id={"dom": peer_at(step)},
                device_id_type=MESH,
            ).start()
            return carry

        lax.fori_loop(1, count, send, 0, unroll=True)

    my_tile = my_w * nz + my_z

    def strip_z(i, strips):
        block = strips.at[pl.ds(my_tile, 1), pl.ds(0, 5)]
        group_send(2 * i, nz, lambda step: (my_z + step) % nz * wide + my_w, block)

    def strip_w(i, strips):
        arrived(group_recv.at[2 * i], strips.at[pl.ds(0, nz - 1), pl.ds(0, 5)])
        block = strips.at[pl.ds(my_w * nz, nz), pl.ds(0, 5)]
        group_send(2 * i + 1, wide, lambda step: my_z * wide + (my_w + step) % wide, block)

    def strip_wait(i, strips):
        arrived(group_recv.at[2 * i + 1], strips.at[pl.ds(0, (wide - 1) * nz), pl.ds(0, 5)])

    def halo_copies(i, low_src, low_dst, up_src, up_dst):
        down = pltpu.make_async_remote_copy(
            src_ref=low_src,
            dst_ref=up_dst,
            send_sem=halo_send.at[2 * i],
            recv_sem=halo_recv.at[2 * i],
            device_id={"dom": jnp.maximum(me - 1, 0)},
            device_id_type=MESH,
        )
        up = pltpu.make_async_remote_copy(
            src_ref=up_src,
            dst_ref=low_dst,
            send_sem=halo_send.at[2 * i + 1],
            recv_sem=halo_recv.at[2 * i + 1],
            device_id={"dom": jnp.minimum(me + 1, n - 1)},
            device_id_type=MESH,
        )
        return down, up

    def halo_start(copies):
        @pl.when(me > 0)
        def _():
            copies[0].start()

        @pl.when(me < n - 1)
        def _():
            copies[1].start()

    def halo_recv_wait(copies):
        @pl.when(me < n - 1)
        def _():
            copies[0].wait_recv()

        @pl.when(me > 0)
        def _():
            copies[1].wait_recv()

    def halo_send_wait(copies):
        @pl.when(me > 0)
        def _():
            copies[0].wait_send()

        @pl.when(me < n - 1)
        def _():
            copies[1].wait_send()

    def line_halo(i, s):
        return halo_copies(
            i,
            s.at[:, pl.ds(OWN, LINE)],
            s.at[:, pl.ds(0, LINE)],
            s.at[:, pl.ds(OWN + 3 * LINE, LINE)],
            s.at[:, pl.ds(UPPER, LINE)],
        )

    def spread(staged, dst, first):
        def body(cf, carry):
            for a in range(AX):
                put(dst, pl.ds(first + cf * 8 + a, RD, stride=LINE), staged[cf, a])
            return carry

        lax.fori_loop(0, 10, body, 0)

    def collect(src, staged, stations):
        def body(cf, carry):
            for a in stations:
                staged[cf, a] = get(src, pl.ds(cf * 8 + a, RD, stride=LINE))
            return carry

        lax.fori_loop(0, 10, body, 0)

    group8 = lane8 // 8 % 8

    def by_field(x):
        turned = jnp.zeros((8, 128), F32)
        for delta in range(-7, 8):
            moved = x if delta == 0 else pltpu.roll(rolled(x, 8 * delta), -delta % 8, 0)
            turned = jnp.where(group8 - row8 == delta, moved, turned)
        return turned

    def make_strip(s, strips):
        def body(r, acc):
            base = pl.multiple_of(OWN + r * LINE, 8)
            part = jnp.zeros((8, 128), F32)
            for cf in range(10):
                ends = jnp.where(
                    lane8 == 0,
                    s[0, pl.ds(base + cf * 8, 8), :],
                    s[s.shape[0] - 1, pl.ds(base + cf * 8, 8), :],
                )
                part = jnp.where(lane8 // 2 == cf * 4, rolled(ends, cf * 8 + 1), part)
            part = pltpu.roll(part, 2 * r, 1)
            return jnp.where(lane8 % 8 // 2 == r, part, acc)

        tile = lax.fori_loop(0, RD, body, jnp.zeros((8, 128), F32), unroll=True)
        strips[my_tile] = by_field(jnp.where(lane8 < 40, tile, rolled(tile, 24)))

    angle = jnp.broadcast_to(phase_ref[0], (8, 128))
    cos_value, sin_value = jnp.cos(angle), jnp.sin(angle)

    def name_faces():
        def body(face, carry):
            owner, slot = owner_ref[face], slot_ref[face]
            side, line = face // (AX * RD), face % (AX * RD)
            face_tile[face] = owner % wide * nz + owner // wide
            face_shift[face] = 2 * (line - slot) + 1 - 2 * side + 128
            return carry

        lax.fori_loop(0, 2 * AX * RD, body, 0, unroll=True)

    def make_inflow(strips, stations):
        partner = jnp.zeros((8, 128), F32)
        for a in stations:
            for side in range(2):
                for r in range(RD):
                    face = side * AX * RD + a * RD + r
                    entry = strips[face_tile[face]]
                    moved = pltpu.roll(entry, face_shift[face], 1)
                    here = lane8 % 64 == a * 8 + 2 * r + 1 - side
                    partner = jnp.where(here, moved, partner)
        other = rolled(partner, 64)
        plus = (lane8 < 64) == (lane8 % 2 == 1)
        flow = cos_value * partner + jnp.where(plus, sin_value, -sin_value) * other
        flow = by_field(flow)
        return jnp.where(lane8 < 40, flow, rolled(flow, -24))

    def mixes(g, x):
        total = mix_ref[g, 0] * x[0]
        for f in range(1, 5):
            total = total + mix_ref[g, f] * x[f]
        return total

    frequency = frequency_ref[0]
    first_lane = lax.broadcasted_iota(jnp.int32, (8, azi), 1) == 0
    last_lane = lax.broadcasted_iota(jnp.int32, (8, azi), 1) == azi - 1
    row = lax.broadcasted_iota(jnp.int32, (8, azi), 0)

    def sweep(s, emit):
        def body(r, carry):
            base = pl.multiple_of(OWN + r * LINE, 8)
            above = pl.multiple_of(base + LINE + r // 3 * PAD, 8)
            x = [get(s, pl.ds(base + cf * 8, 8)) for cf in range(10)]
            for c in range(2):
                for g in range(5):
                    cf = 5 * c + g
                    mine = x[cf]
                    other = x[5 * (1 - c) + g]
                    turn = frequency * other
                    center = 6.0 * mine + mixes(g, x[5 * c : 5 * c + 5])
                    center = center - turn if c == 0 else center + turn
                    along = jnp.where(row == 7, 0.0, pltpu.roll(mine, 7, 0)) + jnp.where(
                        row == 0, 0.0, pltpu.roll(mine, 1, 0)
                    )
                    lines = get(s, pl.ds(base - LINE + cf * 8, 8)) + get(
                        s, pl.ds(above + cf * 8, 8)
                    )
                    after = jnp.where(last_lane, 0.0, pltpu.roll(mine, azi - 1, 1))
                    before = jnp.where(first_lane, 0.0, pltpu.roll(mine, 1, 1))
                    at = pl.multiple_of(r * LINE, 8) + cf * 8
                    image = center - (along + lines + (after + before))
                    emit(at, mine, get(source, pl.ds(at, 8)) - image)
            return carry

        lax.fori_loop(0, RD, body, 0)

    def add_inflow(strips, dst, first, scale, stations):
        flow = scale * make_inflow(strips, stations)
        last = dst.shape[0] - 1

        def body(r, carry):
            here = pltpu.roll(flow, 127 - 2 * r, 1)
            for cf in range(10):
                rows = pl.ds(pl.multiple_of(first + r * LINE, 8) + cf * 8, 8)
                ends = rolled(here, -cf * 8)
                dst[0, rows, :] = dst[0, rows, :] + jnp.where(lane8 == 0, ends, 0.0)
                dst[last, rows, :] = dst[last, rows, :] + jnp.where(lane8 == 127, ends, 0.0)
            return carry

        lax.fori_loop(0, RD, body, 0, unroll=True)

    def forward(s, out):
        halves = []
        for c in range(2):
            blocks = [
                get(s, pl.ds(OWN + r * LINE + c * 40 + 7 * x, 8, stride=8))
                for r in range(RD)
                for x in range(2)
            ]
            halves.append(jnp.concatenate(blocks, axis=0))
        re, im = ([h[:, a * quarter : (a + 1) * quarter] for a in range(4)] for h in halves)
        se, de, so, do = re[0] + re[2], re[0] - re[2], re[1] + re[3], re[1] - re[3]
        te, ue, to, uo = im[0] + im[2], im[0] - im[2], im[1] + im[3], im[1] - im[3]
        classes = [(se + so, te + to), (de + uo, ue - do), (se - so, te - to), (de - uo, ue + do)]
        modes = [None] * MODES
        for b, (yr, yi) in enumerate(classes):
            y = jnp.concatenate(
                [jnp.concatenate([yr, yi], axis=0), jnp.concatenate([yi, -yr], axis=0)], axis=1
            )
            z = dot3((ahead[0, b], ahead[1, b]), split(y), ((1,), (1,)))
            modes[b], modes[4 + b] = z[:n], z[n:]
        for f in range(5):
            part = rolled(modes[0], -f)
            for j in range(1, MODES):
                part = jnp.where(lane % 8 == j, rolled(modes[j], j - f), part)
            out[pl.ds(f, n, stride=8), :] = part

    def cycle_weight(g, f):
        return jnp.where(lane // 8 % 2 == 0, cycle_ref[g, 0, f], cycle_ref[g, 1, f])

    block = lane // 16 % 4

    def filtered(modes):
        blended = []
        for g in range(5):
            total = cycle_weight(g, 0) * modes[0]
            for f in range(1, 5):
                total = total + cycle_weight(g, f) * modes[f]
            blended.append(total)
        for r in range(RD):
            part = rolled(blended[0], -16 * r)
            for g in range(1, 4):
                part = jnp.where(block == g, rolled(blended[g], 16 * (g - r)), part)
            packed[0, pl.ds(r, n, stride=RD), :] = part
            packed[1, pl.ds(r, n, stride=RD), :] = rolled(blended[4], -16 * r)
        x = jnp.concatenate([packed[0], packed[1]], axis=1)
        radial = dot3((basis_hi[...], basis_lo[...]), split(x))
        radial = radial * gain_rows[...]
        back_r = dot3((turned_hi[...], turned_lo[...]), split(radial))
        packed[0] = back_r[:, :128]
        packed[1] = back_r[:, 128:]
        lines0 = [packed[0, pl.ds(r, n, stride=RD), :] for r in range(RD)]
        lines1 = [packed[1, pl.ds(r, n, stride=RD), :] for r in range(RD)]
        result = []
        for g in range(5):
            lines, place = (lines0, g) if g < 4 else (lines1, 0)
            part = rolled(lines[0], -16 * place)
            for r in range(1, RD):
                part = jnp.where(block == r, rolled(lines[r], 16 * (r - place)), part)
            result.append(part)
        return result

    def inverse(modes):
        spread_modes = [modes[pl.ds(g, n, stride=8), :] for g in range(5)]
        z = []
        for j in range(MODES):
            part = rolled(spread_modes[0], -j)
            for g in range(1, 5):
                part = jnp.where(lane % 8 == g, rolled(spread_modes[g], g - j), part)
            z.append(part)
        v = []
        for b in range(4):
            turned = jnp.concatenate([z[b], z[4 + b]], axis=0).T
            y = jnp.concatenate(
                [turned, jnp.concatenate([-turned[64:], turned[:64]], axis=0)], axis=1
            )
            v.append(dot3(split(y), (back[0, b], back[1, b])))
        s, d, p, q = v[0] + v[2], v[0] - v[2], v[1] + v[3], v[1] - v[3]
        iq = jnp.concatenate([-q[64:], q[:64]], axis=0)
        points = jnp.concatenate([s + p, d + iq, s - p, d - iq], axis=1)
        for c in range(2):
            for r in range(RD):
                put(
                    ghosts,
                    pl.ds(r * 32 + c * 16, 16),
                    points[c * 64 + r * 16 : c * 64 + r * 16 + 16],
                )

    def add_ghosts(dst, first, values, start, scale):
        for c in range(2):
            for x in range(2):
                rows = pl.ds(first + c * 40 + 7 * x, 5, stride=8)
                ghost = get(values, pl.ds(start + c * 16 + x * 8, 8))[:5]
                put(dst, rows, get(dst, rows) + scale * ghost)

    seventh = 1.0 / 7.0
    middle = range(1, AX - 1)
    ends = (0, AX - 1)
    loads[0].wait()
    spread(stage, s0, OWN)
    for s in (s0, s1):
        put(s, pl.ds(OWN + RD * LINE, PAD), jnp.zeros((PAD, azi), F32))

    @pl.when(me == 0)
    def _():
        for s in (s0, s1):
            put(s, pl.ds(0, LINE), jnp.zeros((LINE, azi), F32))

    @pl.when(me == n - 1)
    def _():
        for s in (s0, s1):
            put(s, pl.ds(UPPER, LINE), jnp.zeros((LINE, azi), F32))

    make_strip(s0, strips0)
    loads[1].wait()
    forward(s0, modes_out)
    loads[2].wait()
    spread(stage_source, source, 0)
    loads[3].wait()
    whole = basis[...]
    basis_hi[...], basis_lo[...] = split(whole)
    turned_hi[...], turned_lo[...] = split(whole.T)
    loads[4].wait()
    rows0 = [gain[x, g] for c in range(2) for g in range(4) for x in range(2)]
    rows1 = [gain[x, 4] for c in range(2) for g in range(4) for x in range(2)]
    gain_rows[:, :128] = jnp.concatenate(rows0, axis=0).T
    gain_rows[:, 128:] = jnp.concatenate(rows1, axis=0).T
    loads[5].wait()
    name_faces()

    pl.semaphore_wait(barrier, n - 1)
    strip_z(0, strips0)
    exchange(0, modes_out, modes_in)
    halo0 = line_halo(0, s0)
    halo_start(halo0)
    strip_w(0, strips0)

    exchange_wait(0, modes_in)
    first = filtered([modes_in[pl.ds(f, n, stride=8), :] for f in range(5)])
    for g in range(5):
        first_out[pl.ds(g, n, stride=8), :] = first[g]
    exchange(2, first_out, first_in)

    def emit_base(at, mine, value):
        put(s1, pl.ds(OWN + at, 8), mine + value * seventh)

    halo_recv_wait(halo0)
    sweep(s0, emit_base)

    strip_wait(0, strips0)
    add_inflow(strips0, s1, OWN, seventh, ends)
    forward(s1, late_out)
    exchange(1, late_out, late_in)
    add_inflow(strips0, s1, OWN, seventh, middle)

    exchange_wait(2, first_in)
    inverse(first_in)

    def own_ghosts(r, carry):
        add_ghosts(s1, OWN + r * LINE, ghosts, r * 32, seventh)
        return carry

    lax.fori_loop(0, RD, own_ghosts, 0, unroll=True)
    make_strip(s1, strips1)
    strip_z(1, strips1)
    halo1 = line_halo(1, s1)
    halo_start(halo1)

    exchange_wait(1, late_in)
    second = filtered(
        [
            late_in[pl.ds(f, n, stride=8), :] + seventh * first_out[pl.ds(f, n, stride=8), :]
            for f in range(5)
        ]
    )
    for g in range(5):
        second_out[pl.ds(g, n, stride=8), :] = second[g]
    exchange(3, second_out, second_in)
    strip_w(1, strips1)

    def emit_residual(at, mine, value):
        put(res, pl.ds(at, 8), value)

    halo_recv_wait(halo1)
    sweep(s1, emit_residual)
    strip_wait(1, strips1)
    add_inflow(strips1, res, 0, 1.0, range(AX))

    def relax(i, carry):
        at = pl.multiple_of(i * 16, 8)
        rows = pl.ds(at, 16)
        put(source, rows, get(s1, pl.ds(OWN + at, 16)) + get(res, rows) * seventh)
        return carry

    lax.fori_loop(0, RD * LINE // 16, relax, 0, unroll=4)
    collect(res, residual, middle)
    collect(source, relaxed, middle)

    exchange_wait(3, second_in)
    inverse(second_in)

    def last_ghosts(r, carry):
        add_ghosts(res, r * LINE, ghosts, r * 32, 1.0)
        add_ghosts(source, r * LINE, ghosts, r * 32, seventh)
        return carry

    lax.fori_loop(0, RD, last_ghosts, 0, unroll=True)
    collect(res, residual, ends)
    collect(source, relaxed, ends)

    for i, out in enumerate((modes_out, late_out, first_out, second_out)):
        arrived(all_send.at[i], out.at[pl.ds(0, (n - 1) * 5)])
    for i, strips in enumerate((strips0, strips1)):
        arrived(group_sent.at[2 * i], strips.at[pl.ds(0, nz - 1), pl.ds(0, 5)])
        arrived(group_sent.at[2 * i + 1], strips.at[pl.ds(0, (wide - 1) * nz), pl.ds(0, 5)])
    halo_send_wait(halo0)
    halo_send_wait(halo1)


def write_kernel(relaxed, residual, relaxed_hbm, residual_hbm, sem):
    copies = [
        pltpu.make_async_copy(relaxed, relaxed_hbm, sem.at[0]),
        pltpu.make_async_copy(residual, residual_hbm, sem.at[1]),
    ]
    for copy in copies:
        copy.start()
    for copy in copies:
        copy.wait()


def on_device(
    n,
    initial_state,
    source,
    field_coupling,
    frequency,
    phase_angle,
    face_owner,
    face_slot,
    radial_basis,
    cycle_coupling,
    cycle_gain,
):
    azi = MODES * n
    rad = RD * n
    quarter = azi // 4
    ahead, back = fourier_tables(n)
    shape = (10, AX, RD, azi)
    hbm = pl.BlockSpec(memory_space=pl.ANY)
    smem = pl.BlockSpec(memory_space=pltpu.SMEM)
    vmem = pltpu.VMEM
    peers = (n * 8, 128)
    relaxed, residual = pl.pallas_call(
        functools.partial(kernel, n, 8 if n >= 64 else 4),
        out_shape=(vmem(shape, F32), vmem(shape, F32)),
        in_specs=[hbm] * 6 + [smem] * 6,
        out_specs=(pl.BlockSpec(memory_space=vmem), pl.BlockSpec(memory_space=vmem)),
        scratch_shapes=[
            vmem(shape, F32),
            vmem(shape, F32),
            vmem((2, 5, MODES, rad), F32),
            vmem((rad, rad), F32),
            vmem((2, 4, quarter, 2 * quarter), BF16),
            vmem((2, 4, 2 * quarter, quarter), BF16),
            vmem((azi // 128, ROWS, 128), F32),
            vmem((azi // 128, ROWS, 128), F32),
            vmem((azi // 128, RD * LINE, 128), F32),
            vmem((azi // 128, RD * LINE, 128), F32),
            vmem((rad, rad), BF16),
            vmem((rad, rad), BF16),
            vmem((rad, rad), BF16),
            vmem((rad, rad), BF16),
            vmem((rad, 256), F32),
            vmem((n, 8, 128), F32),
            vmem((n, 8, 128), F32),
            *[vmem(peers, F32) for _ in range(8)],
            vmem((2, rad, 128), F32),
            vmem((azi // 128, RD * 32, 128), F32),
            pltpu.SMEM((2 * AX * RD,), jnp.int32),
            pltpu.SMEM((2 * AX * RD,), jnp.int32),
            pltpu.SemaphoreType.DMA((6,)),
            pltpu.SemaphoreType.DMA((4,)),
            pltpu.SemaphoreType.DMA((4,)),
            pltpu.SemaphoreType.DMA((4,)),
            pltpu.SemaphoreType.DMA((4,)),
            pltpu.SemaphoreType.DMA((4,)),
            pltpu.SemaphoreType.DMA((4,)),
        ],
        compiler_params=pltpu.CompilerParams(
            collective_id=0, has_side_effects=True, vmem_limit_bytes=62 * 1024 * 1024
        ),
    )(
        initial_state,
        source,
        jnp.transpose(cycle_gain, (0, 1, 3, 2)),
        radial_basis,
        jnp.asarray(ahead),
        jnp.asarray(back),
        field_coupling,
        frequency,
        phase_angle,
        face_owner.reshape(-1),
        face_slot,
        jnp.transpose(cycle_coupling, (1, 0, 2)),
    )
    return pl.pallas_call(
        write_kernel,
        out_shape=(jax.ShapeDtypeStruct(shape, F32), jax.ShapeDtypeStruct(shape, F32)),
        in_specs=[hbm, hbm],
        out_specs=(hbm, hbm),
        scratch_shapes=[pltpu.SemaphoreType.DMA((2,))],
        compiler_params=pltpu.CompilerParams(vmem_limit_bytes=4 * 1024 * 1024),
    )(relaxed, residual)


def solution(mesh):
    P = jax.sharding.PartitionSpec
    state = P("ibpa", None, "dom", None)
    in_specs = (
        state,
        state,
        P(),
        P(),
        P("ibpa"),
        P("dom", None),
        P("dom"),
        P(),
        P(),
        P(None, None, None, "dom"),
    )
    return jax.shard_map(
        functools.partial(on_device, mesh.shape["dom"]),
        mesh=mesh,
        in_specs=in_specs,
        out_specs=(state, state),
        check_vma=False,
    )
```

```python
import functools

import jax
import jax.numpy as jnp
import ml_dtypes
import numpy as np
from jax import lax
from jax.experimental import pallas as pl
from jax.experimental.pallas import tpu as pltpu

F32 = jnp.float32
BF16 = jnp.bfloat16
AX = 8
RD = 4
MODES = 8
LINE = 80
OWN = LINE
PAD = 24
UPPER = OWN + RD * LINE + PAD
ROWS = UPPER + LINE
MESH = pl.DeviceIdType.MESH


@functools.lru_cache(None)
def fourier_tables(count):
    azi = MODES * count
    quarter = azi // 4
    kk, e = np.arange(quarter) // count, np.arange(quarter) % count
    k = 2 * e + kk
    t = np.arange(quarter)
    ahead, back = [], []
    for b in range(4):
        angle = ((4 * k + b)[:, None] * t[None, :]) % azi * (2 * np.pi / azi)
        ahead.append(np.concatenate([np.cos(angle), np.sin(angle)], axis=1))
        back.append(np.concatenate([np.cos(angle), np.sin(angle)], axis=0) / azi)

    def split(x):
        x = x.astype(np.float32)
        hi = x.astype(ml_dtypes.bfloat16)
        lo = (x - hi.astype(np.float32)).astype(ml_dtypes.bfloat16)
        return np.stack([hi, lo])

    return split(np.stack(ahead)), split(np.stack(back))


def split(x):
    hi = x.astype(BF16)
    return hi, (x - hi.astype(F32)).astype(BF16)


def dot3(a, b, contract=((1,), (0,))):
    dims = (contract, ((), ()))

    def one(u, v):
        return lax.dot_general(u, v, dims, preferred_element_type=F32)

    return one(a[0], b[0]) + (one(a[1], b[0]) + one(a[0], b[1]))


def get(ref, rows):
    return jnp.concatenate([ref[tile, rows, :] for tile in range(ref.shape[0])], axis=1)


def put(ref, rows, value):
    for tile in range(ref.shape[0]):
        ref[tile, rows, :] = value[:, tile * 128 : (tile + 1) * 128]


def rolled(x, shift):
    shift = shift % 128
    return x if shift == 0 else pltpu.roll(x, shift, 1)


def kernel(
    n,
    wide,
    state_hbm,
    source_hbm,
    gain_hbm,
    basis_hbm,
    ahead_hbm,
    back_hbm,
    mix_ref,
    frequency_ref,
    phase_ref,
    owner_ref,
    slot_ref,
    cycle_ref,
    relaxed,
    residual,
    stage,
    stage_source,
    gain,
    basis,
    ahead,
    back,
    s0,
    s1,
    source,
    res,
    basis_hi,
    basis_lo,
    turned_hi,
    turned_lo,
    gain_rows,
    strips0,
    strips1,
    modes_out,
    modes_in,
    late_out,
    late_in,
    first_out,
    first_in,
    second_out,
    second_in,
    packed,
    ghosts,
    face_tile,
    face_shift,
    load_sem,
    all_send,
    all_recv,
    group_sent,
    group_recv,
    halo_send,
    halo_recv,
):
    azi = MODES * n
    quarter = azi // 4
    rad = RD * n
    nz = n // wide
    me = lax.axis_index("dom")
    my_z, my_w = me // wide, me % wide
    barrier = pltpu.get_barrier_semaphore()

    lane = lax.broadcasted_iota(jnp.int32, (1, 128), 1)
    row8 = lax.broadcasted_iota(jnp.int32, (8, 128), 0)
    lane8 = lax.broadcasted_iota(jnp.int32, (8, 128), 1)

    def peer_of(i):
        return (me + n // 2 + (i % 2) * ((i + 1) // 2) - (1 - i % 2) * (i // 2)) % n

    def greet(step, carry):
        pl.semaphore_signal(
            barrier, inc=1, device_id={"dom": peer_of(step)}, device_id_type=MESH
        )
        return carry

    lax.fori_loop(0, n - 1, greet, 0, unroll=True)

    def load(i, src, dst):
        return pltpu.make_async_copy(src, dst, load_sem.at[i])

    loads = [
        load(0, state_hbm, stage),
        load(1, ahead_hbm, ahead),
        load(2, source_hbm, stage_source),
        load(3, basis_hbm, basis),
        load(4, gain_hbm, gain),
        load(5, back_hbm, back),
    ]
    for copy in loads:
        copy.start()

    def send_all(i, src_of, dst):
        def send(step, carry):
            peer = peer_of(step)
            pltpu.make_async_remote_copy(
                src_ref=src_of(peer),
                dst_ref=dst,
                send_sem=all_send.at[i],
                recv_sem=all_recv.at[i],
                device_id={"dom": peer},
                device_id_type=MESH,
            ).start()
            return carry

        lax.fori_loop(0, n - 1, send, 0, unroll=True)

    def tile_rows(device, count):
        return pl.ds(pl.multiple_of(device * 8, 8), count)

    def exchange(i, out, into):
        send_all(i, lambda peer: out.at[tile_rows(peer, 5)], into.at[tile_rows(me, 5)])
        into[tile_rows(me, 8), :] = out[tile_rows(me, 8), :]

    def arrived(sem, ref):
        pltpu.make_async_copy(ref, ref, sem).wait()

    def exchange_wait(i, into):
        arrived(all_recv.at[i], into.at[pl.ds(0, (n - 1) * 5)])

    def group_send(i, count, peer_at, block):
        def send(step, carry):
            pltpu.make_async_remote_copy(
                src_ref=block,
                dst_ref=block,
                send_sem=group_sent.at[i],
                recv_sem=group_recv.at[i],
                device_id={"dom": peer_at(step)},
                device_id_type=MESH,
            ).start()
            return carry

        lax.fori_loop(1, count, send, 0, unroll=True)

    my_tile = my_w * nz + my_z

    def strip_z(i, strips):
        block = strips.at[pl.ds(my_tile, 1), pl.ds(0, 5)]
        group_send(2 * i, nz, lambda step: (my_z + step) % nz * wide + my_w, block)

    def strip_w(i, strips):
        arrived(group_recv.at[2 * i], strips.at[pl.ds(0, nz - 1), pl.ds(0, 5)])
        block = strips.at[pl.ds(my_w * nz, nz), pl.ds(0, 5)]
        group_send(2 * i + 1, wide, lambda step: my_z * wide + (my_w + step) % wide, block)

    def strip_wait(i, strips):
        arrived(group_recv.at[2 * i + 1], strips.at[pl.ds(0, (wide - 1) * nz), pl.ds(0, 5)])

    def halo_copies(i, low_src, low_dst, up_src, up_dst):
        down = pltpu.make_async_remote_copy(
            src_ref=low_src,
            dst_ref=up_dst,
            send_sem=halo_send.at[2 * i],
            recv_sem=halo_recv.at[2 * i],
            device_id={"dom": jnp.maximum(me - 1, 0)},
            device_id_type=MESH,
        )
        up = pltpu.make_async_remote_copy(
            src_ref=up_src,
            dst_ref=low_dst,
            send_sem=halo_send.at[2 * i + 1],
            recv_sem=halo_recv.at[2 * i + 1],
            device_id={"dom": jnp.minimum(me + 1, n - 1)},
            device_id_type=MESH,
        )
        return down, up

    def halo_start(copies):
        @pl.when(me > 0)
        def _():
            copies[0].start()

        @pl.when(me < n - 1)
        def _():
            copies[1].start()

    def halo_recv_wait(copies):
        @pl.when(me < n - 1)
        def _():
            copies[0].wait_recv()

        @pl.when(me > 0)
        def _():
            copies[1].wait_recv()

    def halo_send_wait(copies):
        @pl.when(me > 0)
        def _():
            copies[0].wait_send()

        @pl.when(me < n - 1)
        def _():
            copies[1].wait_send()

    def line_halo(i, s):
        return halo_copies(
            i,
            s.at[:, pl.ds(OWN, LINE)],
            s.at[:, pl.ds(0, LINE)],
            s.at[:, pl.ds(OWN + 3 * LINE, LINE)],
            s.at[:, pl.ds(UPPER, LINE)],
        )

    def spread(staged, dst, first):
        def body(cf, carry):
            for a in range(AX):
                put(dst, pl.ds(first + cf * 8 + a, RD, stride=LINE), staged[cf, a])
            return carry

        lax.fori_loop(0, 10, body, 0)

    def collect(src, staged, stations):
        def body(cf, carry):
            for a in stations:
                staged[cf, a] = get(src, pl.ds(cf * 8 + a, RD, stride=LINE))
            return carry

        lax.fori_loop(0, 10, body, 0, unroll=True)

    group8 = lane8 // 8 % 8

    def by_field(x):
        turned = jnp.zeros((8, 128), F32)
        for delta in range(-7, 8):
            moved = x if delta == 0 else pltpu.roll(rolled(x, 8 * delta), -delta % 8, 0)
            turned = jnp.where(group8 - row8 == delta, moved, turned)
        return turned

    def make_strip(s, strips):
        def body(r, acc):
            base = pl.multiple_of(OWN + r * LINE, 8)
            part = jnp.zeros((8, 128), F32)
            for cf in range(10):
                ends = jnp.where(
                    lane8 == 0,
                    s[0, pl.ds(base + cf * 8, 8), :],
                    s[s.shape[0] - 1, pl.ds(base + cf * 8, 8), :],
                )
                part = jnp.where(lane8 // 2 == cf * 4, rolled(ends, cf * 8 + 1), part)
            part = pltpu.roll(part, 2 * r, 1)
            return jnp.where(lane8 % 8 // 2 == r, part, acc)

        tile = lax.fori_loop(0, RD, body, jnp.zeros((8, 128), F32), unroll=True)
        strips[my_tile] = by_field(jnp.where(lane8 < 40, tile, rolled(tile, 24)))

    angle = jnp.broadcast_to(phase_ref[0], (8, 128))
    cos_value, sin_value = jnp.cos(angle), jnp.sin(angle)

    def name_faces():
        def body(face, carry):
            owner, slot = owner_ref[face], slot_ref[face]
            side, line = face // (AX * RD), face % (AX * RD)
            face_tile[face] = owner % wide * nz + owner // wide
            face_shift[face] = 2 * (line - slot) + 1 - 2 * side + 128
            return carry

        lax.fori_loop(0, 2 * AX * RD, body, 0, unroll=True)

    def make_inflow(strips, stations):
        partner = jnp.zeros((8, 128), F32)
        for a in stations:
            for side in range(2):
                for r in range(RD):
                    face = side * AX * RD + a * RD + r
                    entry = strips[face_tile[face]]
                    moved = pltpu.roll(entry, face_shift[face], 1)
                    here = lane8 % 64 == a * 8 + 2 * r + 1 - side
                    partner = jnp.where(here, moved, partner)
        other = rolled(partner, 64)
        plus = (lane8 < 64) == (lane8 % 2 == 1)
        flow = cos_value * partner + jnp.where(plus, sin_value, -sin_value) * other
        flow = by_field(flow)
        return jnp.where(lane8 < 40, flow, rolled(flow, -24))

    def mixes(g, x):
        total = mix_ref[g, 0] * x[0]
        for f in range(1, 5):
            total = total + mix_ref[g, f] * x[f]
        return total

    frequency = frequency_ref[0]
    first_lane = lax.broadcasted_iota(jnp.int32, (8, azi), 1) == 0
    last_lane = lax.broadcasted_iota(jnp.int32, (8, azi), 1) == azi - 1
    row = lax.broadcasted_iota(jnp.int32, (8, azi), 0)

    def sweep(s, emit):
        def body(r, carry):
            base = pl.multiple_of(OWN + r * LINE, 8)
            above = pl.multiple_of(base + LINE + r // 3 * PAD, 8)
            x = [get(s, pl.ds(base + cf * 8, 8)) for cf in range(10)]
            for c in range(2):
                for g in range(5):
                    cf = 5 * c + g
                    mine = x[cf]
                    other = x[5 * (1 - c) + g]
                    turn = frequency * other
                    center = 6.0 * mine + mixes(g, x[5 * c : 5 * c + 5])
                    center = center - turn if c == 0 else center + turn
                    along = jnp.where(row == 7, 0.0, pltpu.roll(mine, 7, 0)) + jnp.where(
                        row == 0, 0.0, pltpu.roll(mine, 1, 0)
                    )
                    lines = get(s, pl.ds(base - LINE + cf * 8, 8)) + get(
                        s, pl.ds(above + cf * 8, 8)
                    )
                    after = jnp.where(last_lane, 0.0, pltpu.roll(mine, azi - 1, 1))
                    before = jnp.where(first_lane, 0.0, pltpu.roll(mine, 1, 1))
                    at = pl.multiple_of(r * LINE, 8) + cf * 8
                    image = center - (along + lines + (after + before))
                    emit(at, mine, get(source, pl.ds(at, 8)) - image)
            return carry

        lax.fori_loop(0, RD, body, 0)

    def add_inflow(strips, dst, first, scale, stations):
        flow = scale * make_inflow(strips, stations)
        last = dst.shape[0] - 1

        def body(r, carry):
            here = pltpu.roll(flow, 127 - 2 * r, 1)
            for cf in range(10):
                rows = pl.ds(pl.multiple_of(first + r * LINE, 8) + cf * 8, 8)
                ends = rolled(here, -cf * 8)
                dst[0, rows, :] = dst[0, rows, :] + jnp.where(lane8 == 0, ends, 0.0)
                dst[last, rows, :] = dst[last, rows, :] + jnp.where(lane8 == 127, ends, 0.0)
            return carry

        lax.fori_loop(0, RD, body, 0, unroll=True)

    def forward(s, out):
        halves = []
        for c in range(2):
            blocks = [
                get(s, pl.ds(OWN + r * LINE + c * 40 + 7 * x, 8, stride=8))
                for r in range(RD)
                for x in range(2)
            ]
            halves.append(jnp.concatenate(blocks, axis=0))
        re, im = ([h[:, a * quarter : (a + 1) * quarter] for a in range(4)] for h in halves)
        se, de, so, do = re[0] + re[2], re[0] - re[2], re[1] + re[3], re[1] - re[3]
        te, ue, to, uo = im[0] + im[2], im[0] - im[2], im[1] + im[3], im[1] - im[3]
        classes = [(se + so, te + to), (de + uo, ue - do), (se - so, te - to), (de - uo, ue + do)]
        modes = [None] * MODES
        for b, (yr, yi) in enumerate(classes):
            y = jnp.concatenate(
                [jnp.concatenate([yr, yi], axis=0), jnp.concatenate([yi, -yr], axis=0)], axis=1
            )
            z = dot3((ahead[0, b], ahead[1, b]), split(y), ((1,), (1,)))
            modes[b], modes[4 + b] = z[:n], z[n:]
        for f in range(5):
            part = rolled(modes[0], -f)
            for j in range(1, MODES):
                part = jnp.where(lane % 8 == j, rolled(modes[j], j - f), part)
            out[pl.ds(f, n, stride=8), :] = part

    def cycle_weight(g, f):
        return jnp.where(lane // 8 % 2 == 0, cycle_ref[g, 0, f], cycle_ref[g, 1, f])

    block = lane // 16 % 4

    def filtered(modes):
        blended = []
        for g in range(5):
            total = cycle_weight(g, 0) * modes[0]
            for f in range(1, 5):
                total = total + cycle_weight(g, f) * modes[f]
            blended.append(total)
        for r in range(RD):
            part = rolled(blended[0], -16 * r)
            for g in range(1, 4):
                part = jnp.where(block == g, rolled(blended[g], 16 * (g - r)), part)
            packed[0, pl.ds(r, n, stride=RD), :] = part
            packed[1, pl.ds(r, n, stride=RD), :] = rolled(blended[4], -16 * r)
        x = jnp.concatenate([packed[0], packed[1]], axis=1)
        radial = dot3((basis_hi[...], basis_lo[...]), split(x))
        radial = radial * gain_rows[...]
        back_r = dot3((turned_hi[...], turned_lo[...]), split(radial))
        packed[0] = back_r[:, :128]
        packed[1] = back_r[:, 128:]
        lines0 = [packed[0, pl.ds(r, n, stride=RD), :] for r in range(RD)]
        lines1 = [packed[1, pl.ds(r, n, stride=RD), :] for r in range(RD)]
        result = []
        for g in range(5):
            lines, place = (lines0, g) if g < 4 else (lines1, 0)
            part = rolled(lines[0], -16 * place)
            for r in range(1, RD):
                part = jnp.where(block == r, rolled(lines[r], 16 * (r - place)), part)
            result.append(part)
        return result

    def inverse(modes):
        spread_modes = [modes[pl.ds(g, n, stride=8), :] for g in range(5)]
        z = []
        for j in range(MODES):
            part = rolled(spread_modes[0], -j)
            for g in range(1, 5):
                part = jnp.where(lane % 8 == g, rolled(spread_modes[g], g - j), part)
            z.append(part)
        v = []
        for b in range(4):
            turned = jnp.concatenate([z[b], z[4 + b]], axis=0).T
            y = jnp.concatenate(
                [turned, jnp.concatenate([-turned[64:], turned[:64]], axis=0)], axis=1
            )
            v.append(dot3(split(y), (back[0, b], back[1, b])))
        s, d, p, q = v[0] + v[2], v[0] - v[2], v[1] + v[3], v[1] - v[3]
        iq = jnp.concatenate([-q[64:], q[:64]], axis=0)
        points = jnp.concatenate([s + p, d + iq, s - p, d - iq], axis=1)
        for c in range(2):
            for r in range(RD):
                put(
                    ghosts,
                    pl.ds(r * 32 + c * 16, 16),
                    points[c * 64 + r * 16 : c * 64 + r * 16 + 16],
                )

    def add_ghosts(dst, first, values, start, scale):
        for c in range(2):
            for x in range(2):
                rows = pl.ds(first + c * 40 + 7 * x, 5, stride=8)
                ghost = get(values, pl.ds(start + c * 16 + x * 8, 8))[:5]
                put(dst, rows, get(dst, rows) + scale * ghost)

    seventh = 1.0 / 7.0
    middle = range(1, AX - 1)
    ends = (0, AX - 1)
    loads[0].wait()
    spread(stage, s0, OWN)
    for s in (s0, s1):
        put(s, pl.ds(OWN + RD * LINE, PAD), jnp.zeros((PAD, azi), F32))

    @pl.when(me == 0)
    def _():
        for s in (s0, s1):
            put(s, pl.ds(0, LINE), jnp.zeros((LINE, azi), F32))

    @pl.when(me == n - 1)
    def _():
        for s in (s0, s1):
            put(s, pl.ds(UPPER, LINE), jnp.zeros((LINE, azi), F32))

    make_strip(s0, strips0)
    loads[1].wait()
    forward(s0, modes_out)
    loads[2].wait()
    spread(stage_source, source, 0)
    loads[3].wait()
    whole = basis[...]
    basis_hi[...], basis_lo[...] = split(whole)
    turned_hi[...], turned_lo[...] = split(whole.T)
    loads[4].wait()
    rows0 = [gain[x, g] for c in range(2) for g in range(4) for x in range(2)]
    rows1 = [gain[x, 4] for c in range(2) for g in range(4) for x in range(2)]
    gain_rows[:, :128] = jnp.concatenate(rows0, axis=0).T
    gain_rows[:, 128:] = jnp.concatenate(rows1, axis=0).T
    loads[5].wait()
    name_faces()

    pl.semaphore_wait(barrier, n - 1)
    strip_z(0, strips0)
    exchange(0, modes_out, modes_in)
    halo0 = line_halo(0, s0)
    halo_start(halo0)
    strip_w(0, strips0)

    exchange_wait(0, modes_in)
    first = filtered([modes_in[pl.ds(f, n, stride=8), :] for f in range(5)])
    for g in range(5):
        first_out[pl.ds(g, n, stride=8), :] = first[g]
    exchange(2, first_out, first_in)

    def emit_base(at, mine, value):
        put(s1, pl.ds(OWN + at, 8), mine + value * seventh)

    halo_recv_wait(halo0)
    sweep(s0, emit_base)

    strip_wait(0, strips0)
    add_inflow(strips0, s1, OWN, seventh, ends)
    forward(s1, late_out)
    exchange(1, late_out, late_in)
    add_inflow(strips0, s1, OWN, seventh, middle)

    exchange_wait(2, first_in)
    inverse(first_in)

    def own_ghosts(r, carry):
        add_ghosts(s1, OWN + r * LINE, ghosts, r * 32, seventh)
        return carry

    lax.fori_loop(0, RD, own_ghosts, 0, unroll=True)
    make_strip(s1, strips1)
    strip_z(1, strips1)
    halo1 = line_halo(1, s1)
    halo_start(halo1)

    exchange_wait(1, late_in)
    second = filtered(
        [
            late_in[pl.ds(f, n, stride=8), :] + seventh * first_out[pl.ds(f, n, stride=8), :]
            for f in range(5)
        ]
    )
    for g in range(5):
        second_out[pl.ds(g, n, stride=8), :] = second[g]
    exchange(3, second_out, second_in)
    strip_w(1, strips1)

    def emit_residual(at, mine, value):
        put(res, pl.ds(at, 8), value)

    halo_recv_wait(halo1)
    sweep(s1, emit_residual)
    strip_wait(1, strips1)
    add_inflow(strips1, res, 0, 1.0, range(AX))

    def relax(i, carry):
        at = pl.multiple_of(i * 16, 8)
        rows = pl.ds(at, 16)
        put(source, rows, get(s1, pl.ds(OWN + at, 16)) + get(res, rows) * seventh)
        return carry

    lax.fori_loop(0, RD * LINE // 16, relax, 0, unroll=4)
    collect(res, residual, middle)
    collect(source, relaxed, middle)

    exchange_wait(3, second_in)
    inverse(second_in)

    def last_ghosts(r, carry):
        add_ghosts(res, r * LINE, ghosts, r * 32, 1.0)
        add_ghosts(source, r * LINE, ghosts, r * 32, seventh)
        return carry

    lax.fori_loop(0, RD, last_ghosts, 0, unroll=True)
    collect(res, residual, ends)
    collect(source, relaxed, ends)

    for i, out in enumerate((modes_out, late_out, first_out, second_out)):
        arrived(all_send.at[i], out.at[pl.ds(0, (n - 1) * 5)])
    for i, strips in enumerate((strips0, strips1)):
        arrived(group_sent.at[2 * i], strips.at[pl.ds(0, nz - 1), pl.ds(0, 5)])
        arrived(group_sent.at[2 * i + 1], strips.at[pl.ds(0, (wide - 1) * nz), pl.ds(0, 5)])
    halo_send_wait(halo0)
    halo_send_wait(halo1)


def write_kernel(relaxed, residual, relaxed_hbm, residual_hbm, sem):
    copies = []
    for part in range(5):
        fields = pl.ds(2 * part, 2)
        for i, (src, dst) in enumerate(((relaxed, relaxed_hbm), (residual, residual_hbm))):
            copies.append(
                pltpu.make_async_copy(src.at[fields], dst.at[fields], sem.at[2 * part + i])
            )
    for copy in copies:
        copy.start()
    for copy in copies:
        copy.wait()


def on_device(
    n,
    initial_state,
    source,
    field_coupling,
    frequency,
    phase_angle,
    face_owner,
    face_slot,
    radial_basis,
    cycle_coupling,
    cycle_gain,
):
    azi = MODES * n
    rad = RD * n
    quarter = azi // 4
    ahead, back = fourier_tables(n)
    shape = (10, AX, RD, azi)
    hbm = pl.BlockSpec(memory_space=pl.ANY)
    smem = pl.BlockSpec(memory_space=pltpu.SMEM)
    vmem = pltpu.VMEM
    peers = (n * 8, 128)
    relaxed, residual = pl.pallas_call(
        functools.partial(kernel, n, 8 if n >= 64 else 4),
        out_shape=(vmem(shape, F32), vmem(shape, F32)),
        in_specs=[hbm] * 6 + [smem] * 6,
        out_specs=(pl.BlockSpec(memory_space=vmem), pl.BlockSpec(memory_space=vmem)),
        scratch_shapes=[
            vmem(shape, F32),
            vmem(shape, F32),
            vmem((2, 5, MODES, rad), F32),
            vmem((rad, rad), F32),
            vmem((2, 4, quarter, 2 * quarter), BF16),
            vmem((2, 4, 2 * quarter, quarter), BF16),
            vmem((azi // 128, ROWS, 128), F32),
            vmem((azi // 128, ROWS, 128), F32),
            vmem((azi // 128, RD * LINE, 128), F32),
            vmem((azi // 128, RD * LINE, 128), F32),
            vmem((rad, rad), BF16),
            vmem((rad, rad), BF16),
            vmem((rad, rad), BF16),
            vmem((rad, rad), BF16),
            vmem((rad, 256), F32),
            vmem((n, 8, 128), F32),
            vmem((n, 8, 128), F32),
            *[vmem(peers, F32) for _ in range(8)],
            vmem((2, rad, 128), F32),
            vmem((azi // 128, RD * 32, 128), F32),
            pltpu.SMEM((2 * AX * RD,), jnp.int32),
            pltpu.SMEM((2 * AX * RD,), jnp.int32),
            pltpu.SemaphoreType.DMA((6,)),
            pltpu.SemaphoreType.DMA((4,)),
            pltpu.SemaphoreType.DMA((4,)),
            pltpu.SemaphoreType.DMA((4,)),
            pltpu.SemaphoreType.DMA((4,)),
            pltpu.SemaphoreType.DMA((4,)),
            pltpu.SemaphoreType.DMA((4,)),
        ],
        compiler_params=pltpu.CompilerParams(
            collective_id=0, has_side_effects=True, vmem_limit_bytes=62 * 1024 * 1024
        ),
    )(
        initial_state,
        source,
        jnp.transpose(cycle_gain, (0, 1, 3, 2)),
        radial_basis,
        jnp.asarray(ahead),
        jnp.asarray(back),
        field_coupling,
        frequency,
        phase_angle,
        face_owner.reshape(-1),
        face_slot,
        jnp.transpose(cycle_coupling, (1, 0, 2)),
    )
    return pl.pallas_call(
        write_kernel,
        out_shape=(jax.ShapeDtypeStruct(shape, F32), jax.ShapeDtypeStruct(shape, F32)),
        in_specs=[hbm, hbm],
        out_specs=(hbm, hbm),
        scratch_shapes=[pltpu.SemaphoreType.DMA((10,))],
        compiler_params=pltpu.CompilerParams(vmem_limit_bytes=4 * 1024 * 1024),
    )(relaxed, residual)


def solution(mesh):
    P = jax.sharding.PartitionSpec
    state = P("ibpa", None, "dom", None)
    in_specs = (
        state,
        state,
        P(),
        P(),
        P("ibpa"),
        P("dom", None),
        P("dom"),
        P(),
        P(),
        P(None, None, None, "dom"),
    )
    return jax.shard_map(
        functools.partial(on_device, mesh.shape["dom"]),
        mesh=mesh,
        in_specs=in_specs,
        out_specs=(state, state),
        check_vma=False,
    )
```
